32 devices in a mesh: section: 2 (over core), dp: 16 (over z, y, x).
Axes of the slice: x: 2, y: 2, z: 4, core: 2. Of those that a mesh axis runs over, the one named last changes fastest.
Arguments:
- tokens: bfloat16 [2, 2048, 768], P(None, 'dp'), may hold values from -6 to 6
- cotangent: bfloat16 [2, 2048, 768], P(None, 'dp'), may hold values from -6 to 6
- routes: int32 [2, 2, 2048, 2], P('section', None, 'dp'), may hold values from 0 to 15, all different within a row; in each aligned block of 128 rows (0 to 127, 128 to 255, ..., all dimensions but the last counted through in order) at most 32 rows name the same one
- rel_bucket: int32 [1024], replicated, may hold values from 0 to 31, as said below
- query_weight: bfloat16 [2, 768, 768], P('section', 'dp'), may hold values from -0.21875 to 0.21875
- key_weight: bfloat16 [2, 768, 768], P('section', 'dp'), may hold values from -0.21875 to 0.21875
- value_weight: bfloat16 [2, 768, 768], P('section', 'dp'), may hold values from -0.21875 to 0.21875
- output_weight: bfloat16 [2, 768, 768], P('section', 'dp'), may hold values from -0.875 to 0.875
- mixer_gain: bfloat16 [2, 768], P('section', 'dp'), may hold values from 0.5 to 1.5
- feed_gain: bfloat16 [2, 768], P('section', 'dp'), may hold values from 0.5 to 1.5
- router_weight: bfloat16 [2, 768, 16], P('section', 'dp'), may hold values from -0.15625 to 0.15625
- bias_table: bfloat16 [2, 384], P('section', 'dp'), may hold values from -3 to 3
- expert_in: bfloat16 [2, 16, 768, 3072], P('section', 'dp'), may hold values from -0.21875 to 0.21875
- expert_out: bfloat16 [2, 16, 3072, 768], P('section', 'dp'), may hold values from -0.15625 to 0.15625
Outputs:
- activations: bfloat16 [2, 2, 2048, 768], P('section', None, 'dp')
- input_grads: bfloat16 [2, 2, 2048, 768], P('section', None, 'dp')
- grad_query: float32 [2, 768, 768], P('section', 'dp')
- grad_key: float32 [2, 768, 768], P('section', 'dp')
- grad_value: float32 [2, 768, 768], P('section', 'dp')
- grad_output: float32 [2, 768, 768], P('section', 'dp')
- grad_mixer_gain: float32 [2, 768], P('section', 'dp')
- grad_feed_gain: float32 [2, 768], P('section', 'dp')
- grad_router: float32 [2, 768, 16], P('section', 'dp')
- grad_bias: float32 [2, 384], P('section', 'dp')
- grad_expert_in: float32 [2, 16, 768, 3072], P('section', 'dp')
- grad_expert_out: float32 [2, 16, 3072, 768], P('section', 'dp')
The draws below stay inside these ranges and needn't reach their ends.
Inputs may be any that keep to these rules, and one draw needn't show every extreme that they name: `routes`: within the 128 rows of one device for one section and micro-batch, no expert is named by more than 32 rows, a bound that some block reaches; the two experts of a row differ. `rel_bucket`: buckets never fall as the distance grows; distance 0 has bucket 0 and distance 1024 - 1 has bucket 32 - 1.
All inputs are finite; a program needn't handle non-finite values.
Results may differ from the reference program's by a relative error of at most 0.023.
Values may be sent and summed in bfloat16 or wider, within the bound.
No kernel may reach another device: no remote copies, remote signals or barrier semaphores. Data moves between devices by JAX's collectives and lax.ppermute only.
A program may use at most 256 MiB of HBM per device.

```python
import functools
import math
import jax
import jax.numpy as jnp
import numpy as np
from jax import lax

D = 768
HEADS = 12
HEAD_DIM = 64
FF = 3072
BUCKETS = 32
MICRO = 2
TOK_DEV = 128
SEQ_LEN = 1024
TOKENS = 2048
EXPERTS = 16
CAP = 32
N_DP = 16


def draw_rel_bucket(key, part):
    key = jax.random.fold_in(key, 7)
    place = jnp.arange(SEQ_LEN, dtype=jnp.int32)
    pick = jax.random.randint(key, (SEQ_LEN,), 0, 1 << 20, dtype=jnp.int32)
    step = (pick % (place + 1) < 8).astype(jnp.int32)
    step = step.at[0].set(0)
    buckets = jnp.minimum(jnp.cumsum(step), BUCKETS - 1)
    return buckets.at[SEQ_LEN - 1].set(BUCKETS - 1).astype(jnp.int32)


def block_levels(own_key, dims, pieces, smallest, largest):
    factor_of, own = 1.0, jax.random.fold_in(own_key, 6)
    for dim, shards_of in pieces:
        heights = jnp.exp(jax.random.uniform(jax.random.fold_in(own, dim), (shards_of,), jnp.float32, smallest / len(pieces), largest / len(pieces)))
        factor_of = factor_of * jnp.repeat(heights, dims[dim] // shards_of).reshape([-1 if axis == dim else 1 for axis in range(len(dims))])
    return factor_of


def deal_out(stream_key, own, number, rows, number_of, top, bound, lean):
    ranking = jax.random.permutation(stream_key, number_of)
    packed, ordinary = portions_of(number_of, rows * top, bound, lean, True), portions_of(number_of, rows * top, bound, lean, False)
    places = jnp.arange(number_of)

    def named(lengths, rotation):
        used = int((lengths > 0).sum())
        fixed = max(1, used // 4)
        moved = fixed + (places - fixed + rotation * (used - fixed)) % max(1, number_of - fixed)
        return jnp.zeros((number_of,), jnp.int32).at[ranking[jnp.where(places < fixed, places, moved)]].set(jnp.asarray(lengths, jnp.int32))

    lengths = jnp.where(number % 4 == 0, named(packed, number // 4), named(ordinary, number - number // 4 - 1))
    mixed = jax.random.permutation(jax.random.fold_in(own, 3), number_of)
    donor, receiver = mixed[0:number_of // 2 * 2:2], mixed[1:number_of // 2 * 2:2]
    slack = jnp.minimum(lengths[donor] - 1, bound - lengths[receiver]) // 2
    slack = jnp.where((donor == ranking[0]) | (receiver == ranking[0]) | (lengths[receiver] == 0), 0, jnp.maximum(slack, 0))
    moved = jax.random.randint(jax.random.fold_in(own, 4), (number_of // 2,), 0, 1 << 20) % (slack + 1)
    lengths = lengths.at[donor].add(-moved).at[receiver].add(moved)
    labels = jnp.searchsorted(jnp.cumsum(lengths), jnp.arange(rows * top), side="right").astype(jnp.int32)
    grid = labels.reshape(top, rows).T
    grid = grid[jax.random.permutation(jax.random.fold_in(own, 1), rows)]
    rotation = jax.random.randint(jax.random.fold_in(own, 2), (rows, 1), 0, top)
    return jnp.take_along_axis(grid, (jnp.arange(top)[None, :] + rotation) % top, axis=1)


def portions_of(number_of, total, most, slope, full):
    loads = [(1 << 20) // math.isqrt(grade ** slope) + 1 for grade in range(1, number_of + 1)]
    largest = most if full else min(most, max(-(-total // number_of), total * loads[0] // sum(loads)))
    least = 1 if total - largest >= number_of - 1 else 0
    holding, rest = [largest] + [least] * (number_of - 1), total - largest - least * (number_of - 1)
    while rest > 0:
        free = [i for i in range(1, number_of) if holding[i] < largest] or [i for i in range(1, number_of) if holding[i] < most]
        whole, left = sum([loads[i] for i in free]), rest
        for i in free:
            addition = min(most - holding[i], max(1, left * loads[i] // whole), rest)
            holding[i] = holding[i] + addition
            rest = rest - addition
    return np.array(holding)


def noise(key, extent, width, most, shards=(), kind=jnp.bfloat16):
    entries = width * jax.random.normal(key, extent, jnp.float32)
    if shards:
        entries = entries * block_levels(key, extent, shards, -0.22, 0.18)
    return jnp.clip(entries, -most, most).astype(kind)


def setup_inputs(seed: int = 0) -> dict:
    key_list = jax.random.split(jax.random.key(seed), 15)
    tokens = noise(key_list[0], (MICRO, TOKENS, D), 1.0, 6.0, ((1, 16),))
    cotangent = noise(key_list[1], (MICRO, TOKENS, D), 1.0, 6.0, ((1, 16),))
    routes_keys = jax.random.split(jax.random.fold_in(key_list[2], 1), 2 * MICRO * TOKENS // TOK_DEV)
    routes_turns = jax.random.permutation(jax.random.fold_in(key_list[2], 3), 2 * MICRO * TOKENS // TOK_DEV)
    routes = jax.vmap(lambda own, number: deal_out(jax.random.fold_in(key_list[2], 2), own, number, TOK_DEV, EXPERTS, 2, CAP, 2))(routes_keys, routes_turns).reshape((2, MICRO, TOKENS, 2))
    rel_bucket = draw_rel_bucket(jax.random.fold_in(key_list[14], 71), 0)
    query_weight = noise(key_list[4], (2, D, D), D ** -0.5, 0.21875, ((0, 2), (1, 16)))
    key_weight = noise(key_list[5], (2, D, D), D ** -0.5, 0.21875, ((0, 2), (1, 16)))
    value_weight = noise(key_list[6], (2, D, D), D ** -0.5, 0.21875, ((0, 2), (1, 16)))
    output_weight = noise(key_list[7], (2, D, D), (D // 16) ** -0.5, 0.875, ((0, 2), (1, 16)))
    mixer_gain = jnp.clip(1.0 + 0.1 * jax.random.normal(key_list[8], (2, D), jnp.float32), 0.5, 1.5).astype(jnp.bfloat16)
    feed_gain = jnp.clip(1.0 + 0.1 * jax.random.normal(key_list[9], (2, D), jnp.float32), 0.5, 1.5).astype(jnp.bfloat16)
    router_weight = noise(key_list[10], (2, D, EXPERTS), (2 * D) ** -0.5, 0.15625, ((0, 2), (1, 16)))
    bias_table = noise(key_list[11], (2, BUCKETS * HEADS), 0.5, 3.0, ((0, 2), (1, 16)))
    expert_in = noise(key_list[12], (2, EXPERTS, D, FF), D ** -0.5, 0.21875, ((0, 2), (1, 16)))
    expert_out = noise(key_list[13], (2, EXPERTS, FF, D), (FF // 2) ** -0.5, 0.15625, ((0, 2), (1, 16)))
    return {"tokens": tokens, "cotangent": cotangent, "routes": routes, "rel_bucket": rel_bucket, "query_weight": query_weight, "key_weight": key_weight, "value_weight": value_weight, "output_weight": output_weight, "mixer_gain": mixer_gain, "feed_gain": feed_gain, "router_weight": router_weight, "bias_table": bias_table, "expert_in": expert_in, "expert_out": expert_out}


epsilon = 1e-06
score_scale = 0.125
highest = lax.Precision.HIGHEST

@jax.custom_vjp
def low(v):
    return lax.optimization_barrier(v.astype(jnp.bfloat16)).astype(jnp.float32)

@jax.custom_vjp
def low_back(v):
    return v

def low_keep(v):
    return (low(v), None)

def low_pass(kept, grad):
    return (grad,)

def back_keep(v):
    return (v, None)

def back_low(kept, grad):
    return (low(grad),)
low.defvjp(low_keep, low_pass)
low_back.defvjp(back_keep, back_low)

def matrix_product(left, right):
    return jnp.dot(left, right, precision=highest)

def norm_rows(values, gain):
    return values * lax.rsqrt(lax.optimization_barrier(jnp.mean(values * values, axis=-1, keepdims=True)) + epsilon) * gain

def layer(parameters, inputs, route, rel_bucket):
    query_weight, key_weight, value_weight, output_weight, mixer_gain, feed_gain, router_weight, bias_table, expert_in, expert_out = parameters
    normed = low(norm_rows(inputs, mixer_gain))
    query = low_back(low(matrix_product(normed, query_weight)))
    keys = low_back(low(matrix_product(normed, key_weight)))
    values = low_back(low(matrix_product(normed, value_weight)))
    count = inputs.shape[0] // SEQ_LEN
    layout = (count, SEQ_LEN, HEADS, HEAD_DIM)
    places = jnp.arange(SEQ_LEN, dtype=jnp.int32)
    distance = places[:, None] - places[None, :]
    causal = distance >= 0
    bucket_grid = jnp.take(rel_bucket, jnp.clip(distance, 0, SEQ_LEN - 1))
    bias = jnp.transpose(bias_table.reshape(BUCKETS, HEADS)[bucket_grid], (2, 0, 1))

    def attend(block):
        block_query, block_keys, block_values = block
        scores = jnp.einsum('qhd,khd->hqk', block_query, block_keys, precision=highest) * score_scale + bias
        scores = jnp.where(causal[None], low_back(scores), -1e+30)
        weights = jax.nn.softmax(scores, axis=-1)
        return jnp.einsum('hqk,khd->qhd', low(weights), block_values, precision=highest)
    mixed = lax.map(jax.checkpoint(attend), (query.reshape(layout), keys.reshape(layout), values.reshape(layout)))
    mixed = low_back(low(mixed.reshape(-1, D)))
    hidden = inputs + low_back(matrix_product(mixed, output_weight))
    normed_feed = low(norm_rows(hidden, feed_gain))
    logits = low_back(matrix_product(normed_feed, router_weight))
    chances = jax.nn.softmax(logits, axis=-1)
    chosen = jnp.take_along_axis(chances, route, axis=1)
    gate = chosen / lax.optimization_barrier(jnp.sum(chosen, axis=1, keepdims=True))
    flat = route.reshape(-1)
    hot = (flat[:, None] == jnp.arange(EXPERTS, dtype=jnp.int32)[None, :]).astype(jnp.int32)
    place = lax.optimization_barrier(jnp.sum((jnp.cumsum(hot, axis=0) - hot) * hot, axis=1))
    capacity = MICRO * N_DP * CAP
    buffer = jnp.zeros((EXPERTS, capacity, D), jnp.float32).at[flat, place].set(jnp.repeat(normed_feed, 2, axis=0))
    arrived = low_back(buffer)
    before = low_back(jnp.einsum('ecd,edf->ecf', arrived, expert_in, precision=highest))
    activated = low(jax.nn.gelu(before))
    result = low_back(low(jnp.einsum('ecf,efd->ecd', activated, expert_out, precision=highest)))
    back = result[flat, place].reshape(-1, 2, D)
    return hidden + lax.optimization_barrier(jnp.sum(gate[:, :, None] * back, axis=1))

def reference(tokens, cotangent, routes, rel_bucket, query_weight, key_weight, value_weight, output_weight, mixer_gain, feed_gain, router_weight, bias_table, expert_in, expert_out):
    every = (query_weight, key_weight, value_weight, output_weight, mixer_gain, feed_gain, router_weight, bias_table, expert_in, expert_out)

    def parameters_of(section):
        return tuple((array[section].astype(jnp.float32) for array in every))

    def run(section):
        return functools.partial(lambda parameters, inputs, route: layer(parameters, inputs, route, rel_bucket), route=routes[section].reshape(-1, 2))
    first_in = tokens.reshape(-1, D).astype(jnp.float32)
    first_out, first_back = jax.vjp(run(0), parameters_of(0), first_in)
    first_act = first_out.astype(jnp.bfloat16)
    second_out, second_back = jax.vjp(run(1), parameters_of(1), first_act.astype(jnp.float32))
    second_act = second_out.astype(jnp.bfloat16)
    second_grads, second_input = second_back(cotangent.reshape(-1, D).astype(jnp.float32))
    second_input = second_input.astype(jnp.bfloat16)
    first_grads, first_input = first_back(second_input.astype(jnp.float32))
    shape = (MICRO, TOKENS, D)
    activations = jnp.stack([first_act.reshape(shape), second_act.reshape(shape)])
    input_grads = jnp.stack([first_input.astype(jnp.bfloat16).reshape(shape), second_input.reshape(shape)])
    stacked = tuple((jnp.stack([left, right]) for left, right in zip(first_grads, second_grads)))
    return (activations, input_grads, stacked[0], stacked[1], stacked[2], stacked[3], stacked[4], stacked[5], stacked[6], stacked[7], stacked[8], stacked[9])
```

```python
import functools

import jax
import jax.numpy as jnp
from jax import lax
from jax.experimental import pallas as pl
from jax.experimental.pallas import tpu as pltpu
from jax.sharding import PartitionSpec as P

HEADS = 12
HEAD_DIM = 64
BUCKETS = 32
SEQ_LEN = 1024

PAIR = 2 * HEAD_DIM
TILE = 256
BLOCKS = SEQ_LEN // TILE
REACH = SEQ_LEN + TILE

epsilon = 1e-06
score_scale = 0.125
bf16 = jnp.bfloat16
f32 = jnp.float32


def product(left, right):
    return jnp.dot(left, right, preferred_element_type=f32)


def first_contract(left, right):
    return lax.dot_general(left, right, (((0,), (0,)), ((), ())), preferred_element_type=f32)


def last_contract(left, right):
    return lax.dot_general(left, right, (((1,), (1,)), ((), ())), preferred_element_type=f32)


def norm_parts(values):
    scale = lax.rsqrt(jnp.mean(values * values, axis=-1, keepdims=True) + epsilon)
    return (values * scale, scale)


def norm_back(delta_out, unit, scale, gain):
    inner = delta_out * gain
    delta_in = scale * (inner - unit * jnp.mean(inner * unit, axis=-1, keepdims=True))
    return (delta_in, jnp.sum(delta_out * unit, axis=0))


def bias_tile(bias_ref, head, step):
    start = SEQ_LEN - TILE - TILE * step
    line = bias_ref[head : head + 1, start : start + 2 * TILE]
    spread = jnp.broadcast_to(line, (TILE, 2 * TILE))
    return pltpu.roll(spread, TILE + 1, 1, stride=1, stride_axis=0)[:, :TILE]


def block_scores(qkv_ref, tiles, head, block):
    low = HEAD_DIM * head
    seen = TILE * (block + 1)
    query = qkv_ref[TILE * block : seen, low : low + HEAD_DIM]
    key = qkv_ref[0:seen, PAIR + low : PAIR + low + HEAD_DIM]
    raw = last_contract(query, key) * score_scale
    bias = jnp.concatenate([tiles[head, block - j] for j in range(block + 1)], axis=1)
    rows = lax.broadcasted_iota(jnp.int32, (TILE, seen), 0) + TILE * block
    columns = lax.broadcasted_iota(jnp.int32, (TILE, seen), 1)
    scores = jnp.where(columns <= rows, raw + bias, -1e30)
    top = jnp.max(scores, axis=-1, keepdims=True)
    weights = jnp.exp(scores - top)
    weights = weights * (1.0 / jnp.sum(weights, axis=-1, keepdims=True))
    return query, key, weights


def attend_kernel(qkv_ref, bias_ref, out_ref, tiles):
    for head in range(2):
        low = HEAD_DIM * head
        for step in range(BLOCKS):
            tiles[head, step] = bias_tile(bias_ref, head, step)
        for block in range(BLOCKS):
            seen = TILE * (block + 1)
            _, _, weights = block_scores(qkv_ref, tiles, head, block)
            value = qkv_ref[0:seen, 2 * PAIR + low : 2 * PAIR + low + HEAD_DIM]
            out_ref[TILE * block : seen, low : low + HEAD_DIM] = product(
                weights.astype(bf16), value
            ).astype(bf16)


def attend_back_kernel(qkv_ref, bias_ref, delta_ref, grad_ref, line_ref, tiles, sums, keys, values):
    line_ref[...] = jnp.zeros_like(line_ref)
    for head in range(2):
        low = HEAD_DIM * head
        for step in range(BLOCKS):
            tiles[head, step] = bias_tile(bias_ref, head, step)
            sums[step] = jnp.zeros((TILE, TILE), f32)
        keys[...] = jnp.zeros_like(keys)
        values[...] = jnp.zeros_like(values)
        for block in range(BLOCKS):
            seen = TILE * (block + 1)
            query, key, weights = block_scores(qkv_ref, tiles, head, block)
            value = qkv_ref[0:seen, 2 * PAIR + low : 2 * PAIR + low + HEAD_DIM]
            delta = delta_ref[TILE * block : seen, low : low + HEAD_DIM]
            delta_weights = last_contract(delta, value)
            inner = jnp.sum(weights * delta_weights, axis=-1, keepdims=True)
            delta_scores = (weights * (delta_weights - inner)).astype(bf16)
            grad_ref[TILE * block : seen, low : low + HEAD_DIM] = (
                product(delta_scores, key) * score_scale
            ).astype(bf16)
            keys[0:seen, :] += first_contract(delta_scores, query)
            values[0:seen, :] += first_contract(weights.astype(bf16), delta)
            for j in range(block + 1):
                sums[block - j] += delta_scores[:, TILE * j : TILE * (j + 1)].astype(f32)
        grad_ref[:, PAIR + low : PAIR + low + HEAD_DIM] = (keys[...] * score_scale).astype(bf16)
        grad_ref[:, 2 * PAIR + low : 2 * PAIR + low + HEAD_DIM] = values[...].astype(bf16)
        for step in range(BLOCKS):
            start = SEQ_LEN - TILE - TILE * step
            eight = jnp.zeros((8, 2 * TILE), f32)
            for group in range(TILE // 8):
                part = sums[step, 8 * group : 8 * group + 8, :]
                part = jnp.concatenate([part, jnp.zeros_like(part)], axis=1)
                eight = eight + pltpu.roll(part, TILE - 1 - 8 * group, 1)
            line = eight[0:1]
            for row in range(1, 8):
                line = line + pltpu.roll(eight, 2 * TILE - row, 1)[row : row + 1]
            line_ref[head : head + 1, start : start + 2 * TILE] += line


def attend(qkv, bias):
    return pl.pallas_call(
        attend_kernel,
        out_shape=jax.ShapeDtypeStruct((SEQ_LEN, PAIR), bf16),
        in_specs=[pl.BlockSpec(memory_space=pltpu.VMEM)] * 2,
        out_specs=pl.BlockSpec(memory_space=pltpu.VMEM),
        scratch_shapes=[pltpu.VMEM((2, BLOCKS, TILE, TILE), f32)],
        compiler_params=pltpu.CompilerParams(vmem_limit_bytes=40 * 1024 * 1024),
        cost_estimate=pl.CostEstimate(
            flops=2 * SEQ_LEN * SEQ_LEN * PAIR * 2,
            bytes_accessed=SEQ_LEN * PAIR * 8,
            transcendentals=SEQ_LEN * SEQ_LEN,
        ),
    )(qkv, bias)


def attend_back(qkv, bias, delta):
    return pl.pallas_call(
        attend_back_kernel,
        out_shape=(
            jax.ShapeDtypeStruct((SEQ_LEN, 3 * PAIR), bf16),
            jax.ShapeDtypeStruct((8, REACH), f32),
        ),
        in_specs=[pl.BlockSpec(memory_space=pltpu.VMEM)] * 3,
        out_specs=(pl.BlockSpec(memory_space=pltpu.VMEM),) * 2,
        scratch_shapes=[
            pltpu.VMEM((2, BLOCKS, TILE, TILE), f32),
            pltpu.VMEM((BLOCKS, TILE, TILE), f32),
            pltpu.VMEM((SEQ_LEN, HEAD_DIM), f32),
            pltpu.VMEM((SEQ_LEN, HEAD_DIM), f32),
        ],
        compiler_params=pltpu.CompilerParams(vmem_limit_bytes=40 * 1024 * 1024),
        cost_estimate=pl.CostEstimate(
            flops=5 * SEQ_LEN * SEQ_LEN * PAIR * 2,
            bytes_accessed=SEQ_LEN * PAIR * 16,
            transcendentals=SEQ_LEN * SEQ_LEN,
        ),
    )(qkv, bias, delta)


def on_device(
    tokens,
    cotangent,
    routes,
    rel_bucket,
    query_weight,
    key_weight,
    value_weight,
    output_weight,
    mixer_gain,
    feed_gain,
    router_weight,
    bias_table,
    expert_in,
    expert_out,
):
    core = lax.axis_index("section")
    place_dp = lax.axis_index("dp")
    devices = lax.axis_size("dp")
    micro = tokens.shape[0]
    rows = tokens.shape[1]
    width = tokens.shape[2]
    span = SEQ_LEN // rows
    seat = place_dp % span
    slots = max(2, 4 * rows // devices)
    experts = devices
    share = width // devices
    table_share = BUCKETS * HEADS // devices
    used = HEADS // 2
    lanes = 3 * PAIR
    circles = [list(range(i, i + span)) for i in range(0, devices, span)]
    zero = core == 0

    def swap(value):
        return lax.ppermute(value, "section", [(0, 1), (1, 0)])

    def to_sections(own):
        other = swap(own)
        return jnp.where(zero, own, other), jnp.where(zero, other, own)

    def own_of(values):
        return jnp.where(zero, values[0], values[1]), jnp.where(zero, values[1], values[0])

    def exchange(value):
        return lax.all_to_all(value, "dp", 0, 0, tiled=True)

    def exchange_near(value):
        return lax.all_to_all(value, "dp", 0, 0, tiled=True, axis_index_groups=circles)

    def gather_near(value):
        spread = jnp.broadcast_to(value[None], (span,) + value.shape)
        return exchange_near(spread).reshape(SEQ_LEN, -1)

    def by_pairs(weight):
        padded = jnp.pad(weight, ((0, 0), (0, span * PAIR - width)))
        return jnp.transpose(padded.reshape(share, span, PAIR), (1, 0, 2))

    small = jnp.concatenate(
        [mixer_gain[0], feed_gain[0], router_weight[0].reshape(-1), bias_table[0]]
    )
    small_rows = 8 * (-(-small.shape[0] // (8 * lanes)))
    small_pad = small_rows * lanes - small.shape[0]
    small = jnp.pad(small, (0, small_pad)).reshape(1, small_rows, lanes)
    pairs_weight = jnp.concatenate(
        [by_pairs(query_weight[0]), by_pairs(key_weight[0]), by_pairs(value_weight[0])], axis=2
    )
    pairs_weight = jnp.concatenate(
        [pairs_weight, jnp.broadcast_to(small, (span,) + small.shape[1:])], axis=1
    )
    pairs_weight = jnp.concatenate([pairs_weight] * (devices // span), axis=0)
    front = to_sections(exchange(pairs_weight))
    context = jnp.where(zero, tokens[0], tokens[1])
    target = jnp.where(zero, cotangent[0], cotangent[1])
    full_first = gather_near(context)
    output_full = to_sections(
        exchange(jnp.broadcast_to(output_weight, (devices, share, width))).reshape(width, width)
    )
    inner_full = to_sections(expert_in[0, 0])
    outer_full = to_sections(expert_out[0, 0])
    route_mine, route_theirs = own_of((routes[0, 0], routes[0, 1]))
    route_other = swap(route_theirs)
    route_full = (
        jnp.where(zero, route_mine, route_other),
        jnp.where(zero, route_other, route_mine),
    )

    bucket_numbers = jnp.arange(BUCKETS, dtype=jnp.int32)
    reverse = jnp.concatenate([rel_bucket[::-1], jnp.full((TILE,), -1, jnp.int32)])
    bucket_hot = (bucket_numbers[:, None] == reverse[None, :]).astype(f32)
    slot_index = jnp.arange(experts * slots, dtype=jnp.int32)
    expert_index = jnp.arange(experts, dtype=jnp.int32)

    sections = []
    for section in range(2):
        block = front[section]
        attention = block[:, :share].reshape(width, lanes)
        flat_small = block[:, share:].reshape(devices, small_rows * lanes)
        cut = [share, 2 * share, (2 + experts) * share, (2 + experts) * share + table_share]
        gain_mixer = flat_small[:, : cut[0]].reshape(width).astype(f32)
        gain_feed = flat_small[:, cut[0] : cut[1]].reshape(width).astype(f32)
        router = flat_small[:, cut[1] : cut[2]].reshape(width, experts)
        table = flat_small[:, cut[2] : cut[3]].reshape(BUCKETS, HEADS).astype(f32)
        table = jnp.pad(table, ((0, 0), (0, 2 * span - HEADS)))
        mine = lax.dynamic_slice_in_dim(table, 2 * seat, 2, axis=1)
        bias = lax.dot_general(
            mine, bucket_hot, (((0,), (0,)), ((), ())), precision=lax.Precision.HIGHEST
        )
        bias = jnp.pad(bias, ((0, 6), (0, 0)))
        route = route_full[section]
        flat = route.reshape(-1)
        hot = (flat[:, None] == expert_index[None, :]).astype(jnp.int32)
        place = jnp.sum((jnp.cumsum(hot, axis=0) - hot) * hot, axis=1)
        spot = (flat * slots + place).reshape(rows, 2)
        placings = [
            (slot_index[:, None] == spot[:, c][None, :]).astype(bf16) for c in range(2)
        ]
        choose = (route[:, :, None] == expert_index[None, None, :]).astype(f32)
        sections.append(
            {
                "attention": attention,
                "gain_mixer": gain_mixer,
                "gain_feed": gain_feed,
                "router": router,
                "bias": bias,
                "placings": placings,
                "placing": placings[0] + placings[1],
                "choose": choose,
                "output": output_full[section],
                "inner": inner_full[section],
                "outer": outer_full[section],
            }
        )

    def dispatch(p, values):
        out = product(p["placing"], values).astype(bf16)
        return exchange(out.reshape(experts, slots, width)).reshape(experts * slots, width)

    def collect(p, returned):
        return [first_contract(p["placings"][c], returned) for c in range(2)]

    def mixer(p, full, own):
        unit, _ = norm_parts(full.astype(f32))
        normed = (unit * p["gain_mixer"]).astype(bf16)
        qkv = product(normed, p["attention"]).astype(bf16)
        heads = attend(qkv, p["bias"])
        mixed = exchange_near(heads.reshape(span, rows, PAIR))
        mixed = jnp.transpose(mixed[:used], (1, 0, 2)).reshape(rows, width)
        hidden = own.astype(f32) + product(mixed, p["output"])
        unit_feed, scale_feed = norm_parts(hidden)
        normed_feed = (unit_feed * p["gain_feed"]).astype(bf16)
        chances = jax.nn.softmax(product(normed_feed, p["router"]), axis=-1)
        chosen = jnp.sum(chances[:, None, :] * p["choose"], axis=-1)
        gate = chosen / jnp.sum(chosen, axis=1, keepdims=True)
        return {
            "own": own,
            "normed": normed,
            "qkv": qkv,
            "mixed": mixed,
            "hidden": hidden,
            "unit_feed": unit_feed,
            "scale_feed": scale_feed,
            "normed_feed": normed_feed,
            "chances": chances,
            "chosen": chosen,
            "gate": gate,
        }

    def finish(cache, back):
        gate = cache["gate"]
        return (cache["hidden"] + (gate[:, 0:1] * back[0] + gate[:, 1:2] * back[1])).astype(bf16)

    def mixer_back(p, cache, delta_feed, delta_gate, delta_out):
        chosen, chances = cache["chosen"], cache["chances"]
        total = jnp.sum(chosen, axis=1, keepdims=True)
        delta_chosen = delta_gate / total - jnp.sum(
            delta_gate * chosen, axis=1, keepdims=True
        ) / (total * total)
        delta_chances = jnp.sum(delta_chosen[:, :, None] * p["choose"], axis=1)
        delta_logits = (
            chances * (delta_chances - jnp.sum(chances * delta_chances, axis=-1, keepdims=True))
        ).astype(bf16)
        sum_router = first_contract(cache["normed_feed"], delta_logits)
        delta_feed = delta_feed + last_contract(delta_logits, p["router"])
        delta_hidden, sum_feed = norm_back(
            delta_feed, cache["unit_feed"], cache["scale_feed"], p["gain_feed"]
        )
        delta_hidden = delta_hidden + delta_out
        delta_branch = delta_hidden.astype(bf16)
        sum_output = first_contract(cache["mixed"], delta_branch)
        delta_mixed = last_contract(delta_branch, p["output"]).astype(bf16)
        delta_mixed = jnp.pad(delta_mixed, ((0, 0), (0, span * PAIR - width)))
        delta_mixed = jnp.transpose(delta_mixed.reshape(rows, span, PAIR), (1, 0, 2))
        delta_heads = exchange_near(delta_mixed).reshape(SEQ_LEN, PAIR)
        delta_qkv, line = attend_back(cache["qkv"], p["bias"], delta_heads)
        parts = last_contract(delta_qkv, p["attention"]).astype(bf16)
        parts = exchange_near(parts.reshape(span, rows, width))
        delta_normed = jnp.sum(parts.astype(f32), axis=0)
        unit, scale = norm_parts(cache["own"].astype(f32))
        delta_in, sum_mixer = norm_back(delta_normed, unit, scale, p["gain_mixer"])
        delta_in = (delta_in + delta_hidden).astype(bf16)
        sum_attention = first_contract(cache["normed"], delta_qkv)
        sum_table = lax.dot_general(
            bucket_hot, line[:2], (((1,), (1,)), ((), ())), precision=lax.Precision.HIGHEST
        )
        sum_table = lax.dynamic_update_slice_in_dim(
            jnp.zeros((BUCKETS, 2 * span), f32), sum_table, 2 * seat, axis=1
        )[:, :HEADS]
        blocks = jnp.concatenate(
            [
                sum_mixer.reshape(devices, share),
                sum_feed.reshape(devices, share),
                sum_router.reshape(devices, share * experts),
                sum_table.reshape(devices, table_share),
                jnp.zeros((devices, small_pad), f32),
            ],
            axis=1,
        ).reshape(devices, small_rows, lanes)
        sums = jnp.concatenate([sum_attention.reshape(devices, share, lanes), blocks], axis=1)
        return delta_in, sums.astype(bf16), sum_output.astype(bf16)

    p0, p1 = sections
    cache0 = mixer(p0, full_first, context)
    arrived0 = dispatch(p0, cache0["normed_feed"])
    before0 = product(arrived0, p0["inner"])
    activated0 = jax.nn.gelu(before0).astype(bf16)
    result0 = product(activated0, p0["outer"]).astype(bf16)
    back0 = collect(p0, exchange(result0.reshape(experts, slots, width)).reshape(-1, width))
    output0 = finish(cache0, back0)

    arrived_target = dispatch(p1, target)
    delta_act = last_contract(arrived_target, p1["outer"])
    cache1 = mixer(p1, gather_near(output0), output0)
    arrived1 = dispatch(p1, cache1["normed_feed"])
    gate_slots = sum(
        jnp.sum(p1["placings"][c].astype(f32) * cache1["gate"][:, c][None, :], axis=1)
        for c in range(2)
    )
    gate_slots = exchange(gate_slots.reshape(experts, slots)).reshape(-1, 1)
    before1 = product(arrived1, p1["inner"])
    activated1, gelu_back1 = jax.vjp(jax.nn.gelu, before1)
    activated1 = activated1.astype(bf16)
    delta_before1 = gelu_back1(delta_act)[0]
    leaving1 = last_contract(delta_before1.astype(bf16), p1["inner"]).astype(bf16)
    result1 = product(activated1, p1["outer"]).astype(bf16)
    inner_gate = jnp.sum(arrived_target.astype(f32) * result1.astype(f32), axis=-1)
    home1 = collect(p1, exchange(leaving1.reshape(experts, slots, width)).reshape(-1, width))
    inner_gate = exchange(inner_gate.reshape(experts, slots)).reshape(-1)
    delta_gate1 = jnp.stack(
        [
            jnp.sum(p1["placings"][c].astype(f32) * inner_gate[:, None], axis=0)
            for c in range(2)
        ],
        axis=1,
    )
    gate1 = cache1["gate"]
    delta_feed1 = gate1[:, 0:1] * home1[0] + gate1[:, 1:2] * home1[1]
    delta_in1, sums1, sum_output1 = mixer_back(
        p1, cache1, delta_feed1, delta_gate1, target.astype(f32)
    )
    back1 = collect(p1, exchange(result1.reshape(experts, slots, width)).reshape(-1, width))
    output1 = finish(cache1, back1)
    operands1 = (
        activated1,
        (gate_slots * arrived_target.astype(f32)).astype(bf16),
        arrived1,
        (gate_slots * delta_before1).astype(bf16),
    )

    delta_out0 = delta_in1.astype(f32)
    gate0 = cache0["gate"]
    delta_back = [(gate0[:, c : c + 1] * delta_out0).astype(bf16) for c in range(2)]
    outgoing = product(p0["placings"][0], delta_back[0]) + product(p0["placings"][1], delta_back[1])
    arrived_delta = exchange(
        outgoing.astype(bf16).reshape(experts, slots, width)
    ).reshape(-1, width)
    _, gelu_back0 = jax.vjp(jax.nn.gelu, before0)
    delta_before0 = gelu_back0(last_contract(arrived_delta, p0["outer"]))[0].astype(bf16)
    leaving0 = last_contract(delta_before0, p0["inner"]).astype(bf16)
    home0 = collect(p0, exchange(leaving0.reshape(experts, slots, width)).reshape(-1, width))
    delta_gate0 = jnp.stack([jnp.sum(delta_out0 * back0[c], axis=-1) for c in range(2)], axis=1)
    delta_in0, sums0, sum_output0 = mixer_back(
        p0, cache0, home0[0] + home0[1], delta_gate0, delta_out0
    )
    operands0 = (activated0, arrived_delta, arrived0, delta_before0)

    totals = []
    joined = []
    for left, right in zip(operands0, operands1):
        mine, theirs = own_of((left, right))
        joined.append(jnp.concatenate([mine, swap(theirs)], axis=0))
    grad_outer = first_contract(joined[0], joined[1])
    grad_inner = first_contract(joined[2], joined[3])

    def reduced(first, second):
        mine, theirs = own_of((first, second))
        both = (mine.astype(f32) + swap(theirs).astype(f32)).astype(bf16)
        return exchange(both).astype(f32)

    sums = reduced(sums0, sums1)
    attention_sums = sums[:, :share].reshape(devices // span, span, share, 3, PAIR)
    attention_sums = jnp.sum(attention_sums, axis=0)[:used]
    attention_sums = jnp.transpose(attention_sums, (2, 1, 0, 3)).reshape(3, share, width)
    small_sums = jnp.sum(sums[:, share:], axis=0).reshape(-1)
    totals = [small_sums[:share], small_sums[share : 2 * share]]
    totals.append(small_sums[2 * share : (2 + experts) * share].reshape(share, experts))
    end = (2 + experts) * share
    totals.append(small_sums[end : end + table_share])
    output_sums = reduced(
        sum_output0.reshape(devices, share, width), sum_output1.reshape(devices, share, width)
    )
    output_sums = jnp.sum(output_sums, axis=0)

    def by_micro(first, second):
        mine, theirs = own_of((first, second))
        other = swap(theirs)
        return jnp.stack([jnp.where(zero, mine, other), jnp.where(zero, other, mine)])[None]

    return (
        by_micro(output0, output1),
        by_micro(delta_in0, delta_in1),
        attention_sums[0][None],
        attention_sums[1][None],
        attention_sums[2][None],
        output_sums[None],
        totals[0][None],
        totals[1][None],
        totals[2][None],
        totals[3][None],
        grad_inner[None, None],
        grad_outer[None, None],
    )


def solution(mesh):
    in_specs = (
        P(None, "dp", None),
        P(None, "dp", None),
        P("section", None, "dp", None),
        P(),
        P("section", "dp", None),
        P("section", "dp", None),
        P("section", "dp", None),
        P("section", "dp", None),
        P("section", "dp"),
        P("section", "dp"),
        P("section", "dp", None),
        P("section", "dp"),
        P("section", "dp", None, None),
        P("section", "dp", None, None),
    )
    out_specs = (
        P("section", None, "dp", None),
        P("section", None, "dp", None),
        P("section", "dp", None),
        P("section", "dp", None),
        P("section", "dp", None),
        P("section", "dp", None),
        P("section", "dp"),
        P("section", "dp"),
        P("section", "dp", None),
        P("section", "dp"),
        P("section", "dp", None, None),
        P("section", "dp", None, None),
    )
    return jax.shard_map(
        on_device, mesh=mesh, in_specs=in_specs, out_specs=out_specs, check_vma=False
    )
```

```python
import jax
import jax.numpy as jnp
from jax import lax
from jax.experimental import pallas as pl
from jax.experimental.pallas import tpu as pltpu
from jax.sharding import PartitionSpec as P

HEADS = 12
HEAD_DIM = 64
BUCKETS = 32
SEQ_LEN = 1024

PAIR = 2 * HEAD_DIM
TILE = 256
BLOCKS = SEQ_LEN // TILE
REACH = SEQ_LEN + TILE

epsilon = 1e-06
score_scale = 0.125
bf16 = jnp.bfloat16
f32 = jnp.float32


def product(left, right):
    return jnp.dot(left, right, preferred_element_type=f32)


def first_contract(left, right):
    return lax.dot_general(left, right, (((0,), (0,)), ((), ())), preferred_element_type=f32)


def last_contract(left, right):
    return lax.dot_general(left, right, (((1,), (1,)), ((), ())), preferred_element_type=f32)


def norm_parts(values):
    scale = lax.rsqrt(jnp.mean(values * values, axis=-1, keepdims=True) + epsilon)
    return (values * scale, scale)


def norm_back(delta_out, unit, scale, gain):
    inner = delta_out * gain
    delta_in = scale * (inner - unit * jnp.mean(inner * unit, axis=-1, keepdims=True))
    return (delta_in, jnp.sum(delta_out * unit, axis=0))


def bias_tile(bias_ref, head, step):
    start = SEQ_LEN - TILE - TILE * step
    line = bias_ref[head : head + 1, start : start + 2 * TILE]
    spread = jnp.broadcast_to(line, (TILE, 2 * TILE))
    return pltpu.roll(spread, TILE + 1, 1, stride=1, stride_axis=0)[:, :TILE]


def block_scores(qkv_ref, tiles, head, block):
    low = HEAD_DIM * head
    seen = TILE * (block + 1)
    query = qkv_ref[TILE * block : seen, low : low + HEAD_DIM]
    key = qkv_ref[0:seen, PAIR + low : PAIR + low + HEAD_DIM]
    raw = last_contract(query, key) * score_scale
    bias = jnp.concatenate([tiles[head, block - j] for j in range(block + 1)], axis=1)
    rows = lax.broadcasted_iota(jnp.int32, (TILE, seen), 0) + TILE * block
    columns = lax.broadcasted_iota(jnp.int32, (TILE, seen), 1)
    scores = jnp.where(columns <= rows, raw + bias, -1e30)
    top = jnp.max(scores, axis=-1, keepdims=True)
    weights = jnp.exp(scores - top)
    weights = weights * (1.0 / jnp.sum(weights, axis=-1, keepdims=True))
    return query, key, weights


def attend_kernel(qkv_ref, bias_ref, out_ref, tiles):
    for head in range(2):
        low = HEAD_DIM * head
        for step in range(BLOCKS):
            tiles[head, step] = bias_tile(bias_ref, head, step)
        for block in range(BLOCKS):
            seen = TILE * (block + 1)
            _, _, weights = block_scores(qkv_ref, tiles, head, block)
            value = qkv_ref[0:seen, 2 * PAIR + low : 2 * PAIR + low + HEAD_DIM]
            out_ref[TILE * block : seen, low : low + HEAD_DIM] = product(
                weights.astype(bf16), value
            ).astype(bf16)


def attend_back_kernel(qkv_ref, bias_ref, delta_ref, grad_ref, line_ref, tiles, sums, keys, values):
    line_ref[...] = jnp.zeros_like(line_ref)
    for head in range(2):
        low = HEAD_DIM * head
        for step in range(BLOCKS):
            tiles[head, step] = bias_tile(bias_ref, head, step)
            sums[step] = jnp.zeros((TILE, TILE), f32)
        keys[...] = jnp.zeros_like(keys)
        values[...] = jnp.zeros_like(values)
        for block in range(BLOCKS):
            seen = TILE * (block + 1)
            query, key, weights = block_scores(qkv_ref, tiles, head, block)
            value = qkv_ref[0:seen, 2 * PAIR + low : 2 * PAIR + low + HEAD_DIM]
            delta = delta_ref[TILE * block : seen, low : low + HEAD_DIM]
            delta_weights = last_contract(delta, value)
            inner = jnp.sum(weights * delta_weights, axis=-1, keepdims=True)
            delta_scores = (weights * (delta_weights - inner)).astype(bf16)
            grad_ref[TILE * block : seen, low : low + HEAD_DIM] = (
                product(delta_scores, key) * score_scale
            ).astype(bf16)
            keys[0:seen, :] += first_contract(delta_scores, query)
            values[0:seen, :] += first_contract(weights.astype(bf16), delta)
            for j in range(block + 1):
                sums[block - j] += delta_scores[:, TILE * j : TILE * (j + 1)].astype(f32)
        grad_ref[:, PAIR + low : PAIR + low + HEAD_DIM] = (keys[...] * score_scale).astype(bf16)
        grad_ref[:, 2 * PAIR + low : 2 * PAIR + low + HEAD_DIM] = values[...].astype(bf16)
        for step in range(BLOCKS):
            start = SEQ_LEN - TILE - TILE * step
            eight = jnp.zeros((8, 2 * TILE), f32)
            for group in range(TILE // 8):
                part = sums[step, 8 * group : 8 * group + 8, :]
                part = jnp.concatenate([part, jnp.zeros_like(part)], axis=1)
                eight = eight + pltpu.roll(part, TILE - 1 - 8 * group, 1)
            line = eight[0:1]
            for row in range(1, 8):
                line = line + pltpu.roll(eight, 2 * TILE - row, 1)[row : row + 1]
            line_ref[head : head + 1, start : start + 2 * TILE] += line


def attend(qkv, bias):
    return pl.pallas_call(
        attend_kernel,
        out_shape=jax.ShapeDtypeStruct((SEQ_LEN, PAIR), bf16),
        in_specs=[pl.BlockSpec(memory_space=pltpu.VMEM)] * 2,
        out_specs=pl.BlockSpec(memory_space=pltpu.VMEM),
        scratch_shapes=[pltpu.VMEM((2, BLOCKS, TILE, TILE), f32)],
        compiler_params=pltpu.CompilerParams(vmem_limit_bytes=40 * 1024 * 1024),
        cost_estimate=pl.CostEstimate(
            flops=48 * SEQ_LEN * SEQ_LEN * PAIR,
            bytes_accessed=SEQ_LEN * PAIR * 8,
            transcendentals=SEQ_LEN * SEQ_LEN,
        ),
    )(qkv, bias)


def attend_back(qkv, bias, delta):
    return pl.pallas_call(
        attend_back_kernel,
        out_shape=(
            jax.ShapeDtypeStruct((SEQ_LEN, 3 * PAIR), bf16),
            jax.ShapeDtypeStruct((8, REACH), f32),
        ),
        in_specs=[pl.BlockSpec(memory_space=pltpu.VMEM)] * 3,
        out_specs=(pl.BlockSpec(memory_space=pltpu.VMEM),) * 2,
        scratch_shapes=[
            pltpu.VMEM((2, BLOCKS, TILE, TILE), f32),
            pltpu.VMEM((BLOCKS, TILE, TILE), f32),
            pltpu.VMEM((SEQ_LEN, HEAD_DIM), f32),
            pltpu.VMEM((SEQ_LEN, HEAD_DIM), f32),
        ],
        compiler_params=pltpu.CompilerParams(vmem_limit_bytes=40 * 1024 * 1024),
        cost_estimate=pl.CostEstimate(
            flops=96 * SEQ_LEN * SEQ_LEN * PAIR,
            bytes_accessed=SEQ_LEN * PAIR * 16,
            transcendentals=SEQ_LEN * SEQ_LEN,
        ),
    )(qkv, bias, delta)


CHUNK = 512
PART = 256
gelu_root = 0.7978845608028654
gelu_cube = 0.044715


def gelu_parts(before):
    square = before * before
    bend = jnp.tanh(gelu_root * before * (1.0 + gelu_cube * square))
    half = 0.5 * (1.0 + bend)
    slope = half + (0.5 * gelu_root) * before * (1.0 - bend * bend) * (
        1.0 + (3.0 * gelu_cube) * square
    )
    return before * half, slope


def add_product(total, value):
    @pl.when(pl.program_id(0) == 0)
    def _():
        total[...] = value

    @pl.when(pl.program_id(0) > 0)
    def _():
        total[...] += value


def pick(choice_ref, refs):
    return jnp.where(choice_ref[0] == 1, refs[0][...], refs[1][...])


def parts_of(value, axis):
    return jnp.split(value, CHUNK // PART, axis=axis)


def forward_kernel(
    choice_ref, in_ref, inner_0, inner_1, outer_0, outer_1, act_ref, slope_ref, out_ref, total
):
    values = in_ref[...]
    inner = parts_of(pick(choice_ref, (inner_0, inner_1)), 1)
    outer = parts_of(pick(choice_ref, (outer_0, outer_1)), 0)
    befores = [product(values, part) for part in inner]
    value = 0.0
    for i, before in enumerate(befores):
        act, slope = gelu_parts(before)
        act = act.astype(bf16)
        act_ref[:, PART * i : PART * (i + 1)] = act
        slope_ref[:, PART * i : PART * (i + 1)] = slope.astype(bf16)
        value = value + product(act, outer[i])
    add_product(total, value)

    @pl.when(pl.program_id(0) == pl.num_programs(0) - 1)
    def _():
        out_ref[...] = total[...].astype(bf16)


def backward_kernel(
    choice_ref, delta_ref, slope_ref, inner_0, inner_1, outer_0, outer_1, pre_ref, out_ref, total
):
    inner = pick(choice_ref, (inner_0, inner_1))
    outer = pick(choice_ref, (outer_0, outer_1))
    pre = last_contract(delta_ref[...], outer) * slope_ref[...].astype(f32)
    pre = pre.astype(bf16)
    pre_ref[...] = pre
    add_product(total, last_contract(pre, inner))

    @pl.when(pl.program_id(0) == pl.num_programs(0) - 1)
    def _():
        out_ref[...] = total[...].astype(bf16)


def both_kernel(
    choice_ref,
    in_ref,
    delta_ref,
    inner_0,
    inner_1,
    outer_0,
    outer_1,
    act_ref,
    pre_ref,
    out_ref,
    back_ref,
    total,
    back,
):
    values, delta = in_ref[...], delta_ref[...]
    inner = parts_of(pick(choice_ref, (inner_0, inner_1)), 1)
    outer = parts_of(pick(choice_ref, (outer_0, outer_1)), 0)
    befores = [product(values, part) for part in inner]
    deltas = [last_contract(delta, part) for part in outer]
    value, value_back = 0.0, 0.0
    for i, before in enumerate(befores):
        act, slope = gelu_parts(before)
        act = act.astype(bf16)
        act_ref[:, PART * i : PART * (i + 1)] = act
        pre = (deltas[i] * slope).astype(bf16)
        pre_ref[:, PART * i : PART * (i + 1)] = pre
        value_back = value_back + last_contract(pre, inner[i])
        value = value + product(act, outer[i])
    add_product(back, value_back)
    add_product(total, value)

    @pl.when(pl.program_id(0) == pl.num_programs(0) - 1)
    def _():
        out_ref[...] = total[...].astype(bf16)
        back_ref[...] = back[...].astype(bf16)


def expert_call(kernel, held, streamed, weights, wide, narrow):
    choice, inner, outer = weights
    rows, width = held[0].shape
    hidden = inner[0].shape[1]
    whole = pl.BlockSpec((rows, width), lambda i, c: (0, 0))
    cut = pl.BlockSpec((rows, CHUNK), lambda i, c: (0, i))
    return pl.pallas_call(
        kernel,
        grid_spec=pltpu.PrefetchScalarGridSpec(
            num_scalar_prefetch=1,
            grid=(hidden // CHUNK,),
            in_specs=[whole] * len(held)
            + [cut] * len(streamed)
            + [
                pl.BlockSpec((width, CHUNK), lambda i, c: (0, i * c[0])),
                pl.BlockSpec((width, CHUNK), lambda i, c: (0, i * (1 - c[0]))),
                pl.BlockSpec((CHUNK, width), lambda i, c: (i * c[0], 0)),
                pl.BlockSpec((CHUNK, width), lambda i, c: (i * (1 - c[0]), 0)),
            ],
            out_specs=[cut] * wide + [whole] * narrow,
            scratch_shapes=[pltpu.VMEM((rows, width), f32)] * narrow,
        ),
        out_shape=[jax.ShapeDtypeStruct((rows, hidden), bf16)] * wide
        + [jax.ShapeDtypeStruct((rows, width), bf16)] * narrow,
        compiler_params=pltpu.CompilerParams(vmem_limit_bytes=48 * 1024 * 1024),
        cost_estimate=pl.CostEstimate(
            flops=12 * narrow * rows * width * hidden,
            bytes_accessed=4 * width * hidden + 2 * rows * hidden * (wide + len(streamed)),
            transcendentals=rows * hidden,
        ),
    )(choice, *held, *streamed, *inner, *outer)


def on_device(
    tokens,
    cotangent,
    routes,
    rel_bucket,
    query_weight,
    key_weight,
    value_weight,
    output_weight,
    mixer_gain,
    feed_gain,
    router_weight,
    bias_table,
    expert_in,
    expert_out,
):
    core = lax.axis_index("section")
    place_dp = lax.axis_index("dp")
    devices = lax.axis_size("dp")
    micro = tokens.shape[0]
    rows = tokens.shape[1]
    width = tokens.shape[2]
    span = SEQ_LEN // rows
    seat = place_dp % span
    slots = max(2, 4 * rows // devices)
    experts = devices
    share = width // devices
    table_share = BUCKETS * HEADS // devices
    used = HEADS // 2
    lanes = 3 * PAIR
    circles = [list(range(i, i + span)) for i in range(0, devices, span)]
    zero = core == 0

    def swap(value):
        return lax.ppermute(value, "section", [(0, 1), (1, 0)])

    def to_sections(own):
        other = swap(own)
        return jnp.where(zero, own, other), jnp.where(zero, other, own)

    def own_of(values):
        return jnp.where(zero, values[0], values[1]), jnp.where(zero, values[1], values[0])

    def after(value, first):
        element = first[(0,) * first.ndim].astype(f32)
        return value + (element * 0.0).astype(value.dtype)

    def exchange(value):
        return lax.all_to_all(value, "dp", 0, 0, tiled=True)

    def exchange_near(value):
        return lax.all_to_all(value, "dp", 0, 0, tiled=True, axis_index_groups=circles)

    def gather_near(value):
        spread = jnp.broadcast_to(value[None], (span,) + value.shape)
        return exchange_near(spread).reshape(SEQ_LEN, -1)

    def by_pairs(values):
        count = values.shape[0]
        padded = jnp.pad(values, ((0, 0), (0, span * PAIR - width)))
        return jnp.transpose(padded.reshape(count, span, PAIR), (1, 0, 2))

    def three_by_pairs(left, middle, right):
        return jnp.concatenate([by_pairs(left), by_pairs(middle), by_pairs(right)], axis=2)

    context = jnp.where(zero, tokens[0], tokens[1])
    target = jnp.where(zero, cotangent[0], cotangent[1])
    full_first = gather_near(context)

    dense_own = lax.all_gather(
        jnp.concatenate(
            [query_weight[0], key_weight[0], value_weight[0], output_weight[0]], axis=1
        ),
        "dp",
        axis=0,
        tiled=True,
    )
    small = jnp.concatenate(
        [mixer_gain[0], feed_gain[0], router_weight[0].reshape(-1), bias_table[0]]
    )
    small_rows = 8 * (-(-small.shape[0] // (8 * lanes)))
    small_pad = small_rows * lanes - small.shape[0]
    small = jnp.pad(small, (0, small_pad)).reshape(1, small_rows, lanes)
    half = share // 2
    pairs_weight = three_by_pairs(query_weight[0], key_weight[0], value_weight[0])
    passed = lax.ppermute(pairs_weight[:, half:], "section", [(0, 1)])
    pairs_weight = jnp.concatenate(
        [
            jnp.where(zero, pairs_weight[:, :half], passed),
            jnp.broadcast_to(small, (span,) + small.shape[1:]),
        ],
        axis=1,
    )
    pairs_weight = jnp.concatenate([pairs_weight] * (devices // span), axis=0)
    pairs_weight, full_first = lax.optimization_barrier((pairs_weight, full_first))
    front = to_sections(exchange(pairs_weight))
    attention_first = jnp.concatenate([front[0][:, :half], front[1][:, :half]], axis=1).reshape(
        width, lanes
    )
    inner_own, outer_own = expert_in[0, 0], expert_out[0, 0]
    inner_other, outer_other = swap(inner_own), swap(outer_own)
    route_mine, route_theirs = own_of((routes[0, 0], routes[0, 1]))
    route_other = swap(route_theirs)
    route_full = (
        jnp.where(zero, route_mine, route_other),
        jnp.where(zero, route_other, route_mine),
    )

    bucket_numbers = jnp.arange(BUCKETS, dtype=jnp.int32)
    reverse = jnp.concatenate([rel_bucket[::-1], jnp.full((TILE,), -1, jnp.int32)])
    bucket_hot = (bucket_numbers[:, None] == reverse[None, :]).astype(f32)
    slot_index = jnp.arange(experts * slots, dtype=jnp.int32)
    expert_index = jnp.arange(experts, dtype=jnp.int32)

    sections = []
    for section in range(2):
        flat_small = front[section][:, half:].reshape(devices, small_rows * lanes)
        cut = [share, 2 * share, (2 + experts) * share, (2 + experts) * share + table_share]
        gain_mixer = flat_small[:, : cut[0]].reshape(width).astype(f32)
        gain_feed = flat_small[:, cut[0] : cut[1]].reshape(width).astype(f32)
        router = flat_small[:, cut[1] : cut[2]].reshape(width, experts)
        table = flat_small[:, cut[2] : cut[3]].reshape(BUCKETS, HEADS).astype(f32)
        table = jnp.pad(table, ((0, 0), (0, 2 * span - HEADS)))
        mine = lax.dynamic_slice_in_dim(table, 2 * seat, 2, axis=1)
        bias = lax.dot_general(
            mine, bucket_hot, (((0,), (0,)), ((), ())), precision=lax.Precision.HIGHEST
        )
        bias = jnp.pad(bias, ((0, 6), (0, 0)))
        route = route_full[section]
        flat = route.reshape(-1)
        hot = (flat[:, None] == expert_index[None, :]).astype(jnp.int32)
        place = jnp.sum((jnp.cumsum(hot, axis=0) - hot) * hot, axis=1)
        spot = (flat * slots + place).reshape(rows, 2)
        placings = [
            (slot_index[:, None] == spot[:, c][None, :]).astype(bf16) for c in range(2)
        ]
        choose = (route[:, :, None] == expert_index[None, None, :]).astype(f32)
        sections.append(
            {
                "gain_mixer": gain_mixer,
                "gain_feed": gain_feed,
                "router": router,
                "bias": bias,
                "placings": placings,
                "placing": placings[0] + placings[1],
                "choose": choose,
                "weights": (
                    (core == section).astype(jnp.int32).reshape(1),
                    (inner_own, inner_other),
                    (outer_own, outer_other),
                ),
            }
        )

    def dispatch(p, values):
        out = product(p["placing"], values).astype(bf16)
        return exchange(out.reshape(experts, slots, width)).reshape(experts * slots, width)

    def rows_from_all(values, route):
        named = jnp.pad(route.astype(bf16), ((0, 0), (0, PAIR - 2)))
        every = lax.all_gather(jnp.concatenate([values, named], axis=1), "dp", axis=0)
        taken = every[:, :, width : width + 2].astype(jnp.int32) == place_dp
        taken = jnp.any(taken, axis=-1).astype(jnp.int32)
        rank = jnp.cumsum(taken, axis=1) - taken
        places = jnp.arange(slots, dtype=jnp.int32)[None, :, None]
        hot = (rank[:, None, :] == places) & (taken[:, None, :] == 1)
        rows_in = jnp.einsum(
            "ksr,krd->ksd", hot.astype(bf16), every[:, :, :width], preferred_element_type=f32
        )
        return rows_in.astype(bf16).reshape(experts * slots, width)

    def collect(p, returned):
        return [first_contract(p["placings"][c], returned) for c in range(2)]

    def with_line(values, line):
        line = line.reshape(experts, slots)
        high = lax.reduce_precision(line, 8, 7)
        line = jnp.concatenate([high, line - high], axis=1).astype(bf16)
        line = jnp.pad(line, ((0, 0), (0, width - 2 * slots)))
        return jnp.concatenate([values.reshape(experts, slots, width), line[:, None]], axis=1)

    def cut_line(values):
        line = values[:, slots, : 2 * slots].astype(f32)
        line = line[:, :slots] + line[:, slots:]
        return values[:, :slots].reshape(experts * slots, width), line.reshape(-1, 1)

    def normed_mixer(p, values):
        unit, _ = norm_parts(values.astype(f32))
        return (unit * p["gain_mixer"]).astype(bf16)

    def mixer(p, qkv, heads, own):
        mixed = exchange_near(heads.reshape(span, rows, PAIR))
        mixed = jnp.transpose(mixed[:used], (1, 0, 2)).reshape(rows, width)
        hidden = own.astype(f32) + product(mixed, p["output"])
        unit_feed, scale_feed = norm_parts(hidden)
        normed_feed = (unit_feed * p["gain_feed"]).astype(bf16)
        chances = jax.nn.softmax(product(normed_feed, p["router"]), axis=-1)
        chosen = jnp.sum(chances[:, None, :] * p["choose"], axis=-1)
        gate = chosen / jnp.sum(chosen, axis=1, keepdims=True)
        return {
            "own": own,
            "qkv": qkv,
            "mixed": mixed,
            "hidden": hidden,
            "unit_feed": unit_feed,
            "scale_feed": scale_feed,
            "normed_feed": normed_feed,
            "chances": chances,
            "chosen": chosen,
            "gate": gate,
        }

    def finish(cache, back):
        gate = cache["gate"]
        return (cache["hidden"] + (gate[:, 0:1] * back[0] + gate[:, 1:2] * back[1])).astype(bf16)

    def mixer_back(p, cache, delta_feed, delta_gate, delta_out, beside):
        chosen, chances = cache["chosen"], cache["chances"]
        total = jnp.sum(chosen, axis=1, keepdims=True)
        delta_chosen = delta_gate / total - jnp.sum(
            delta_gate * chosen, axis=1, keepdims=True
        ) / (total * total)
        delta_chances = jnp.sum(delta_chosen[:, :, None] * p["choose"], axis=1)
        delta_logits = (
            chances * (delta_chances - jnp.sum(chances * delta_chances, axis=-1, keepdims=True))
        ).astype(bf16)
        sum_router = first_contract(cache["normed_feed"], delta_logits)
        delta_feed = delta_feed + last_contract(delta_logits, p["router"])
        delta_hidden, sum_feed = norm_back(
            delta_feed, cache["unit_feed"], cache["scale_feed"], p["gain_feed"]
        )
        delta_hidden = delta_hidden + delta_out
        delta_branch = delta_hidden.astype(bf16)
        delta_mixed = last_contract(delta_branch, p["output"]).astype(bf16)
        delta_heads = exchange_near(by_pairs(delta_mixed)).reshape(SEQ_LEN, PAIR)
        beside = after(beside, delta_heads)
        sum_output = first_contract(cache["mixed"], after(delta_branch, delta_heads))
        delta_qkv, line = attend_back(cache["qkv"], p["bias"], delta_heads)
        parts = exchange_near(delta_qkv.reshape(span, rows, lanes))
        parts = jnp.transpose(parts[:used].reshape(used, rows, 3, PAIR), (1, 2, 0, 3))
        delta_normed = last_contract(parts.reshape(rows, 3 * width), p["qkv"])
        unit, scale = norm_parts(cache["own"].astype(f32))
        delta_in, sum_mixer = norm_back(delta_normed, unit, scale, p["gain_mixer"])
        delta_in = (delta_in + delta_hidden).astype(bf16)
        sum_attention = first_contract(cache["normed"], delta_qkv)
        sum_table = lax.dot_general(
            bucket_hot, line[:2], (((1,), (1,)), ((), ())), precision=lax.Precision.HIGHEST
        )
        sum_table = lax.dynamic_update_slice_in_dim(
            jnp.zeros((BUCKETS, 2 * span), f32), sum_table, 2 * seat, axis=1
        )[:, :HEADS]
        blocks = jnp.concatenate(
            [
                sum_mixer.reshape(devices, share),
                sum_feed.reshape(devices, share),
                sum_router.reshape(devices, share * experts),
                sum_table.reshape(devices, table_share),
                jnp.zeros((devices, small_pad), f32),
            ],
            axis=1,
        ).reshape(devices, small_rows, lanes)
        sums = (
            sum_attention.reshape(devices, share, lanes),
            blocks,
        )
        sums = jnp.concatenate(sums, axis=1)
        return delta_in, sums, sum_output, beside

    def half_columns(sums):
        mine, theirs = own_of((sums[:, : width // 2], sums[:, width // 2 :]))
        return mine + swap(theirs.astype(bf16)).astype(f32)

    p0, p1 = sections
    normed0 = normed_mixer(p0, full_first)
    qkv0 = product(normed0, attention_first).astype(bf16)
    heads0 = attend(qkv0, p0["bias"])
    p0["output"], p1["output"] = to_sections(after(dense_own[:, 3 * width :], heads0))
    cache0 = mixer(p0, qkv0, heads0, context)
    cache0["normed"] = normed0
    arrived0 = dispatch(p0, cache0["normed_feed"])
    arrived_target = rows_from_all(target, route_full[1])
    activated0, slope0, result0 = expert_call(
        forward_kernel, [arrived0], [], p0["weights"], 2, 1
    )
    returned0 = exchange(result0.reshape(experts, slots, width)).reshape(-1, width)
    p0["qkv"], p1["qkv"] = to_sections(after(dense_own[:, : 3 * width], result0))
    back0 = collect(p0, returned0)
    output0 = finish(cache0, back0)

    qkv1 = product(normed_mixer(p1, output0), p1["qkv"]).astype(bf16)
    qkv1 = exchange_near(
        three_by_pairs(qkv1[:, :width], qkv1[:, width : 2 * width], qkv1[:, 2 * width :])
    ).reshape(SEQ_LEN, lanes)
    cache1 = mixer(p1, qkv1, attend(qkv1, p1["bias"]), output0)
    gate1 = cache1["gate"]
    gate_slots = sum(
        jnp.sum(p1["placings"][c].astype(f32) * gate1[:, c][None, :], axis=1) for c in range(2)
    )
    outgoing1 = product(p1["placing"], cache1["normed_feed"]).astype(bf16)
    arrived1, gate_slots = cut_line(exchange(with_line(outgoing1, gate_slots)))
    delta1 = (gate_slots * arrived_target.astype(f32)).astype(bf16)
    full_second = lax.all_gather(
        output0, "dp", axis=0, tiled=True, axis_index_groups=circles
    )
    activated1, before1, result1, leaving1 = expert_call(
        both_kernel, [arrived1, delta1], [], p1["weights"], 2, 2
    )
    cache1["normed"] = normed_mixer(p1, after(full_second, result1))
    inner_gate = jnp.sum(arrived_target.astype(f32) * result1.astype(f32), axis=-1)
    home1, inner_gate = cut_line(exchange(with_line(leaving1, inner_gate)))
    home1 = collect(p1, home1)
    delta_gate1 = jnp.stack(
        [jnp.sum(p1["placings"][c].astype(f32) * inner_gate, axis=0) for c in range(2)], axis=1
    )
    delta_in1, sums1, sum_output1, result1 = mixer_back(
        p1, cache1, home1[0] + home1[1], delta_gate1, target.astype(f32), result1
    )
    back1 = collect(p1, exchange(result1.reshape(experts, slots, width)).reshape(-1, width))
    output1 = finish(cache1, back1)

    delta_out0 = delta_in1.astype(f32)
    gate0 = cache0["gate"]
    delta_back = [(gate0[:, c : c + 1] * delta_out0).astype(bf16) for c in range(2)]
    outgoing = product(p0["placings"][0], delta_back[0]) + product(p0["placings"][1], delta_back[1])
    arrived_delta = exchange(
        outgoing.astype(bf16).reshape(experts, slots, width)
    ).reshape(-1, width)
    output_half1 = lax.psum_scatter(
        half_columns(sum_output1), "dp", scatter_dimension=0, tiled=True
    )
    before0, leaving0 = expert_call(
        backward_kernel, [arrived_delta], [slope0], p0["weights"], 1, 1
    )
    home0 = collect(p0, exchange(leaving0.reshape(experts, slots, width)).reshape(-1, width))
    delta_gate0 = jnp.stack([jnp.sum(delta_out0 * back0[c], axis=-1) for c in range(2)], axis=1)
    delta_in0, sums0, sum_output0, _ = mixer_back(
        p0, cache0, home0[0] + home0[1], delta_gate0, delta_out0, result0
    )
    output_half0 = half_columns(sum_output0).astype(bf16).reshape(devices, share, width // 2)
    output_half0 = jnp.sum(exchange(output_half0).astype(f32), axis=0)

    operands0 = (activated0, arrived_delta, arrived0, before0)
    operands1 = (activated1, delta1, arrived1, before1)
    joined = []
    for left, right in zip(operands0, operands1):
        mine, theirs = own_of((left, right))
        joined.append(jnp.concatenate([mine, swap(theirs)], axis=0))
    grad_outer = first_contract(joined[0], joined[1])
    grad_inner = first_contract(joined[2], joined[3])

    mine, theirs = own_of((sums0, sums1))
    sums = exchange((mine + swap(theirs.astype(bf16)).astype(f32)).astype(bf16)).astype(f32)
    attention_sums = sums[:, :share].reshape(devices // span, span, share, 3, PAIR)
    attention_sums = jnp.sum(attention_sums, axis=0)[:used]
    attention_sums = jnp.transpose(attention_sums, (2, 1, 0, 3)).reshape(3, share, width)
    small_sums = jnp.sum(sums[:, share:], axis=0).reshape(-1)
    mine, theirs = own_of((output_half0, output_half1))
    other = swap(theirs)
    output_sums = jnp.concatenate(
        [jnp.where(zero, mine, other), jnp.where(zero, other, mine)], axis=1
    )
    totals = [small_sums[:share], small_sums[share : 2 * share]]
    totals.append(small_sums[2 * share : (2 + experts) * share].reshape(share, experts))
    end = (2 + experts) * share
    totals.append(small_sums[end : end + table_share])

    def by_micro(first, second):
        mine, theirs = own_of((first, second))
        other = swap(theirs)
        return jnp.stack([jnp.where(zero, mine, other), jnp.where(zero, other, mine)])[None]

    return (
        by_micro(output0, output1),
        by_micro(delta_in0, delta_in1),
        attention_sums[0][None],
        attention_sums[1][None],
        attention_sums[2][None],
        output_sums[None],
        totals[0][None],
        totals[1][None],
        totals[2][None],
        totals[3][None],
        grad_inner[None, None],
        grad_outer[None, None],
    )


def solution(mesh):
    in_specs = (
        P(None, "dp", None),
        P(None, "dp", None),
        P("section", None, "dp", None),
        P(),
        P("section", "dp", None),
        P("section", "dp", None),
        P("section", "dp", None),
        P("section", "dp", None),
        P("section", "dp"),
        P("section", "dp"),
        P("section", "dp", None),
        P("section", "dp"),
        P("section", "dp", None, None),
        P("section", "dp", None, None),
    )
    out_specs = (
        P("section", None, "dp", None),
        P("section", None, "dp", None),
        P("section", "dp", None),
        P("section", "dp", None),
        P("section", "dp", None),
        P("section", "dp", None),
        P("section", "dp"),
        P("section", "dp"),
        P("section", "dp", None),
        P("section", "dp"),
        P("section", "dp", None, None),
        P("section", "dp", None, None),
    )
    return jax.shard_map(
        on_device, mesh=mesh, in_specs=in_specs, out_specs=out_specs, check_vma=False
    )
```

```python
import functools

import jax
import jax.numpy as jnp
from jax import lax
from jax.experimental import pallas as pl
from jax.experimental.pallas import tpu as pltpu
from jax.sharding import PartitionSpec as P

HEADS = 12
HEAD_DIM = 64
BUCKETS = 32
SEQ_LEN = 1024

PAIR = 2 * HEAD_DIM
TILE = 256
BLOCKS = SEQ_LEN // TILE
REACH = SEQ_LEN + TILE

epsilon = 1e-06
score_scale = 0.125
bf16 = jnp.bfloat16
f32 = jnp.float32


def product(left, right):
    return jnp.dot(left, right, preferred_element_type=f32)


def first_contract(left, right):
    return lax.dot_general(left, right, (((0,), (0,)), ((), ())), preferred_element_type=f32)


def last_contract(left, right):
    return lax.dot_general(left, right, (((1,), (1,)), ((), ())), preferred_element_type=f32)


def norm_parts(values):
    scale = lax.rsqrt(jnp.mean(values * values, axis=-1, keepdims=True) + epsilon)
    return (values * scale, scale)


def norm_back(delta_out, unit, scale, gain):
    inner = delta_out * gain
    delta_in = scale * (inner - unit * jnp.mean(inner * unit, axis=-1, keepdims=True))
    return (delta_in, jnp.sum(delta_out * unit, axis=0))


def bias_tile(bias_ref, head, step):
    start = SEQ_LEN - TILE - TILE * step
    line = bias_ref[head : head + 1, start : start + 2 * TILE]
    spread = jnp.broadcast_to(line, (TILE, 2 * TILE))
    return pltpu.roll(spread, TILE + 1, 1, stride=1, stride_axis=0)[:, :TILE]


def block_scores(qkv_ref, tiles, head, block):
    low = HEAD_DIM * head
    seen = TILE * (block + 1)
    query = qkv_ref[TILE * block : seen, low : low + HEAD_DIM]
    key = qkv_ref[0:seen, PAIR + low : PAIR + low + HEAD_DIM]
    raw = last_contract(query, key) * score_scale
    bias = jnp.concatenate([tiles[head, block - j] for j in range(block + 1)], axis=1)
    rows = lax.broadcasted_iota(jnp.int32, (TILE, seen), 0) + TILE * block
    columns = lax.broadcasted_iota(jnp.int32, (TILE, seen), 1)
    scores = jnp.where(columns <= rows, raw + bias, -1e30)
    top = jnp.max(scores, axis=-1, keepdims=True)
    weights = jnp.exp(scores - top)
    weights = weights * (1.0 / jnp.sum(weights, axis=-1, keepdims=True))
    return query, key, weights


def attend_kernel(qkv_ref, bias_ref, out_ref, tiles):
    for head in range(2):
        low = HEAD_DIM * head
        for step in range(BLOCKS):
            tiles[head, step] = bias_tile(bias_ref, head, step)
        for block in range(BLOCKS):
            seen = TILE * (block + 1)
            _, _, weights = block_scores(qkv_ref, tiles, head, block)
            value = qkv_ref[0:seen, 2 * PAIR + low : 2 * PAIR + low + HEAD_DIM]
            out_ref[TILE * block : seen, low : low + HEAD_DIM] = product(
                weights.astype(bf16), value
            ).astype(bf16)


def attend_back_kernel(qkv_ref, bias_ref, delta_ref, grad_ref, line_ref, tiles, sums, keys, values):
    line_ref[...] = jnp.zeros_like(line_ref)
    for head in range(2):
        low = HEAD_DIM * head
        for step in range(BLOCKS):
            tiles[head, step] = bias_tile(bias_ref, head, step)
            sums[step] = jnp.zeros((TILE, TILE), f32)
        keys[...] = jnp.zeros_like(keys)
        values[...] = jnp.zeros_like(values)
        for block in range(BLOCKS):
            seen = TILE * (block + 1)
            query, key, weights = block_scores(qkv_ref, tiles, head, block)
            value = qkv_ref[0:seen, 2 * PAIR + low : 2 * PAIR + low + HEAD_DIM]
            delta = delta_ref[TILE * block : seen, low : low + HEAD_DIM]
            delta_weights = last_contract(delta, value)
            inner = jnp.sum(weights * delta_weights, axis=-1, keepdims=True)
            delta_scores = (weights * (delta_weights - inner)).astype(bf16)
            grad_ref[TILE * block : seen, low : low + HEAD_DIM] = (
                product(delta_scores, key) * score_scale
            ).astype(bf16)
            keys[0:seen, :] += first_contract(delta_scores, query)
            values[0:seen, :] += first_contract(weights.astype(bf16), delta)
            for j in range(block + 1):
                sums[block - j] += delta_scores[:, TILE * j : TILE * (j + 1)].astype(f32)
        grad_ref[:, PAIR + low : PAIR + low + HEAD_DIM] = (keys[...] * score_scale).astype(bf16)
        grad_ref[:, 2 * PAIR + low : 2 * PAIR + low + HEAD_DIM] = values[...].astype(bf16)
        for step in range(BLOCKS):
            start = SEQ_LEN - TILE - TILE * step
            eight = jnp.zeros((8, 2 * TILE), f32)
            for group in range(TILE // 8):
                part = sums[step, 8 * group : 8 * group + 8, :]
                part = jnp.concatenate([part, jnp.zeros_like(part)], axis=1)
                eight = eight + pltpu.roll(part, TILE - 1 - 8 * group, 1)
            line = eight[0:1]
            for row in range(1, 8):
                line = line + pltpu.roll(eight, 2 * TILE - row, 1)[row : row + 1]
            line_ref[head : head + 1, start : start + 2 * TILE] += line


def attend(qkv, bias):
    return pl.pallas_call(
        attend_kernel,
        out_shape=jax.ShapeDtypeStruct((SEQ_LEN, PAIR), bf16),
        in_specs=[pl.BlockSpec(memory_space=pltpu.VMEM)] * 2,
        out_specs=pl.BlockSpec(memory_space=pltpu.VMEM),
        scratch_shapes=[pltpu.VMEM((2, BLOCKS, TILE, TILE), f32)],
        compiler_params=pltpu.CompilerParams(vmem_limit_bytes=40 * 1024 * 1024),
        cost_estimate=pl.CostEstimate(
            flops=48 * SEQ_LEN * SEQ_LEN * PAIR,
            bytes_accessed=SEQ_LEN * PAIR * 8,
            transcendentals=SEQ_LEN * SEQ_LEN,
        ),
    )(qkv, bias)


def attend_back(qkv, bias, delta):
    return pl.pallas_call(
        attend_back_kernel,
        out_shape=(
            jax.ShapeDtypeStruct((SEQ_LEN, 3 * PAIR), bf16),
            jax.ShapeDtypeStruct((8, REACH), f32),
        ),
        in_specs=[pl.BlockSpec(memory_space=pltpu.VMEM)] * 3,
        out_specs=(pl.BlockSpec(memory_space=pltpu.VMEM),) * 2,
        scratch_shapes=[
            pltpu.VMEM((2, BLOCKS, TILE, TILE), f32),
            pltpu.VMEM((BLOCKS, TILE, TILE), f32),
            pltpu.VMEM((SEQ_LEN, HEAD_DIM), f32),
            pltpu.VMEM((SEQ_LEN, HEAD_DIM), f32),
        ],
        compiler_params=pltpu.CompilerParams(vmem_limit_bytes=40 * 1024 * 1024),
        cost_estimate=pl.CostEstimate(
            flops=96 * SEQ_LEN * SEQ_LEN * PAIR,
            bytes_accessed=SEQ_LEN * PAIR * 16,
            transcendentals=SEQ_LEN * SEQ_LEN,
        ),
    )(qkv, bias, delta)


CHUNK = 512
PART = 256
gelu_root = 0.7978845608028654
gelu_cube = 0.044715


def gelu_parts(before):
    square = before * before
    bend = jnp.tanh(gelu_root * before * (1.0 + gelu_cube * square))
    half = 0.5 * (1.0 + bend)
    slope = half + (0.5 * gelu_root) * before * (1.0 - bend * bend) * (
        1.0 + (3.0 * gelu_cube) * square
    )
    return before * half, slope


def add_product(total, value):
    @pl.when(pl.program_id(0) == 0)
    def _():
        total[...] = value

    @pl.when(pl.program_id(0) > 0)
    def _():
        total[...] += value


def pick(choice_ref, refs):
    return jnp.where(choice_ref[0] == 1, refs[0][...], refs[1][...])


def parts_of(value, axis):
    return jnp.split(value, CHUNK // PART, axis=axis)


def forward_kernel(
    choice_ref, in_ref, inner_0, inner_1, outer_0, outer_1, act_ref, slope_ref, out_ref, total
):
    values = in_ref[...]
    inner = parts_of(pick(choice_ref, (inner_0, inner_1)), 1)
    outer = parts_of(pick(choice_ref, (outer_0, outer_1)), 0)
    befores = [product(values, part) for part in inner]
    value = 0.0
    for i, before in enumerate(befores):
        act, slope = gelu_parts(before)
        act = act.astype(bf16)
        act_ref[:, PART * i : PART * (i + 1)] = act
        slope_ref[:, PART * i : PART * (i + 1)] = slope.astype(bf16)
        value = value + product(act, outer[i])
    add_product(total, value)

    @pl.when(pl.program_id(0) == pl.num_programs(0) - 1)
    def _():
        out_ref[...] = total[...].astype(bf16)


def backward_kernel(
    choice_ref, delta_ref, slope_ref, inner_0, inner_1, outer_0, outer_1, pre_ref, out_ref, total
):
    inner = pick(choice_ref, (inner_0, inner_1))
    outer = pick(choice_ref, (outer_0, outer_1))
    pre = last_contract(delta_ref[...], outer) * slope_ref[...].astype(f32)
    pre = pre.astype(bf16)
    pre_ref[...] = pre
    add_product(total, last_contract(pre, inner))

    @pl.when(pl.program_id(0) == pl.num_programs(0) - 1)
    def _():
        out_ref[...] = total[...].astype(bf16)


def both_kernel(
    choice_ref,
    in_ref,
    delta_ref,
    inner_0,
    inner_1,
    outer_0,
    outer_1,
    act_ref,
    pre_ref,
    out_ref,
    back_ref,
    total,
    back,
):
    values, delta = in_ref[...], delta_ref[...]
    inner = parts_of(pick(choice_ref, (inner_0, inner_1)), 1)
    outer = parts_of(pick(choice_ref, (outer_0, outer_1)), 0)
    befores = [product(values, part) for part in inner]
    deltas = [last_contract(delta, part) for part in outer]
    value, value_back = 0.0, 0.0
    for i, before in enumerate(befores):
        act, slope = gelu_parts(before)
        act = act.astype(bf16)
        act_ref[:, PART * i : PART * (i + 1)] = act
        pre = (deltas[i] * slope).astype(bf16)
        pre_ref[:, PART * i : PART * (i + 1)] = pre
        value_back = value_back + last_contract(pre, inner[i])
        value = value + product(act, outer[i])
    add_product(back, value_back)
    add_product(total, value)

    @pl.when(pl.program_id(0) == pl.num_programs(0) - 1)
    def _():
        out_ref[...] = total[...].astype(bf16)
        back_ref[...] = back[...].astype(bf16)


def expert_call(kernel, held, streamed, weights, wide, narrow):
    choice, inner, outer = weights
    rows, width = held[0].shape
    hidden = inner[0].shape[1]
    whole = pl.BlockSpec((rows, width), lambda i, c: (0, 0))
    cut = pl.BlockSpec((rows, CHUNK), lambda i, c: (0, i))
    return pl.pallas_call(
        kernel,
        grid_spec=pltpu.PrefetchScalarGridSpec(
            num_scalar_prefetch=1,
            grid=(hidden // CHUNK,),
            in_specs=[whole] * len(held)
            + [cut] * len(streamed)
            + [
                pl.BlockSpec((width, CHUNK), lambda i, c: (0, i * c[0])),
                pl.BlockSpec((width, CHUNK), lambda i, c: (0, i * (1 - c[0]))),
                pl.BlockSpec((CHUNK, width), lambda i, c: (i * c[0], 0)),
                pl.BlockSpec((CHUNK, width), lambda i, c: (i * (1 - c[0]), 0)),
            ],
            out_specs=[cut] * wide + [whole] * narrow,
            scratch_shapes=[pltpu.VMEM((rows, width), f32)] * narrow,
        ),
        out_shape=[jax.ShapeDtypeStruct((rows, hidden), bf16)] * wide
        + [jax.ShapeDtypeStruct((rows, width), bf16)] * narrow,
        compiler_params=pltpu.CompilerParams(vmem_limit_bytes=48 * 1024 * 1024),
        cost_estimate=pl.CostEstimate(
            flops=12 * narrow * rows * width * hidden,
            bytes_accessed=4 * width * hidden + 2 * rows * hidden * (wide + len(streamed)),
            transcendentals=rows * hidden,
        ),
    )(choice, *held, *streamed, *inner, *outer)


def add_pairs_kernel(span, in_ref, *out_refs):
    share, width = out_refs[0].shape
    for part, out_ref in enumerate(out_refs):
        for pair in range(width // PAIR):
            total = 0.0
            for source in range(pair, in_ref.shape[0], span):
                block = in_ref[source, 0:share, PAIR * part : PAIR * (part + 1)]
                total = total + block.astype(f32)
            out_ref[:, PAIR * pair : PAIR * (pair + 1)] = total


def add_pairs(blocks, span, share):
    return pl.pallas_call(
        functools.partial(add_pairs_kernel, span),
        out_shape=[jax.ShapeDtypeStruct((share, HEADS * HEAD_DIM), f32)] * 3,
        in_specs=[pl.BlockSpec(memory_space=pltpu.VMEM)],
        out_specs=[pl.BlockSpec(memory_space=pltpu.VMEM)] * 3,
        compiler_params=pltpu.CompilerParams(vmem_limit_bytes=32 * 1024 * 1024),
    )(blocks)


def on_device(
    tokens,
    cotangent,
    routes,
    rel_bucket,
    query_weight,
    key_weight,
    value_weight,
    output_weight,
    mixer_gain,
    feed_gain,
    router_weight,
    bias_table,
    expert_in,
    expert_out,
):
    core = lax.axis_index("section")
    place_dp = lax.axis_index("dp")
    devices = lax.axis_size("dp")
    micro = tokens.shape[0]
    rows = tokens.shape[1]
    width = tokens.shape[2]
    span = SEQ_LEN // rows
    seat = place_dp % span
    slots = max(2, 4 * rows // devices)
    experts = devices
    share = width // devices
    table_share = BUCKETS * HEADS // devices
    used = HEADS // 2
    lanes = 3 * PAIR
    circles = [list(range(i, i + span)) for i in range(0, devices, span)]
    zero = core == 0

    def swap(value):
        return lax.ppermute(value, "section", [(0, 1), (1, 0)])

    def to_sections(own):
        other = swap(own)
        return jnp.where(zero, own, other), jnp.where(zero, other, own)

    def own_of(values):
        return jnp.where(zero, values[0], values[1]), jnp.where(zero, values[1], values[0])

    def after(value, first):
        element = first[(0,) * first.ndim].astype(f32)
        return value + (element * 0.0).astype(value.dtype)

    def exchange(value):
        return lax.all_to_all(value, "dp", 0, 0, tiled=True)

    def exchange_near(value):
        return lax.all_to_all(value, "dp", 0, 0, tiled=True, axis_index_groups=circles)

    def gather_near(value):
        spread = jnp.broadcast_to(value[None], (span,) + value.shape)
        return exchange_near(spread).reshape(SEQ_LEN, -1)

    def by_pairs(values):
        count = values.shape[0]
        padded = jnp.pad(values, ((0, 0), (0, span * PAIR - width)))
        return jnp.transpose(padded.reshape(count, span, PAIR), (1, 0, 2))

    def three_by_pairs(left, middle, right):
        return jnp.concatenate([by_pairs(left), by_pairs(middle), by_pairs(right)], axis=2)

    context = jnp.where(zero, tokens[0], tokens[1])
    target = jnp.where(zero, cotangent[0], cotangent[1])
    full_first = gather_near(context)

    dense_own = lax.all_gather(
        jnp.concatenate(
            [query_weight[0], key_weight[0], value_weight[0], output_weight[0]], axis=1
        ),
        "dp",
        axis=0,
        tiled=True,
    )
    small = jnp.concatenate(
        [mixer_gain[0], feed_gain[0], router_weight[0].reshape(-1), bias_table[0]]
    )
    small_rows = 8 * (-(-small.shape[0] // (8 * lanes)))
    small_pad = small_rows * lanes - small.shape[0]
    small = jnp.pad(small, (0, small_pad)).reshape(1, small_rows, lanes)
    half = share // 2
    pairs_weight = three_by_pairs(query_weight[0], key_weight[0], value_weight[0])
    passed = lax.ppermute(pairs_weight[:, half:], "section", [(0, 1)])
    pairs_weight = jnp.concatenate(
        [
            jnp.where(zero, pairs_weight[:, :half], passed),
            jnp.broadcast_to(small, (span,) + small.shape[1:]),
        ],
        axis=1,
    )
    pairs_weight = jnp.concatenate([pairs_weight] * (devices // span), axis=0)
    pairs_weight, full_first = lax.optimization_barrier((pairs_weight, full_first))
    front = to_sections(exchange(pairs_weight))
    attention_first = jnp.concatenate([front[0][:, :half], front[1][:, :half]], axis=1).reshape(
        width, lanes
    )
    inner_own, outer_own = expert_in[0, 0], expert_out[0, 0]
    inner_other, outer_other = swap(inner_own), swap(outer_own)
    route_mine, route_theirs = own_of((routes[0, 0], routes[0, 1]))
    route_other = swap(route_theirs)
    route_full = (
        jnp.where(zero, route_mine, route_other),
        jnp.where(zero, route_other, route_mine),
    )

    bucket_numbers = jnp.arange(BUCKETS, dtype=jnp.int32)
    reverse = jnp.concatenate([rel_bucket[::-1], jnp.full((TILE,), -1, jnp.int32)])
    bucket_hot = (bucket_numbers[:, None] == reverse[None, :]).astype(f32)
    slot_index = jnp.arange(experts * slots, dtype=jnp.int32)
    expert_index = jnp.arange(experts, dtype=jnp.int32)

    sections = []
    for section in range(2):
        flat_small = front[section][:, half:].reshape(devices, small_rows * lanes)
        cut = [share, 2 * share, (2 + experts) * share, (2 + experts) * share + table_share]
        gain_mixer = flat_small[:, : cut[0]].reshape(width).astype(f32)
        gain_feed = flat_small[:, cut[0] : cut[1]].reshape(width).astype(f32)
        router = flat_small[:, cut[1] : cut[2]].reshape(width, experts)
        table = flat_small[:, cut[2] : cut[3]].reshape(BUCKETS, HEADS).astype(f32)
        table = jnp.pad(table, ((0, 0), (0, 2 * span - HEADS)))
        mine = lax.dynamic_slice_in_dim(table, 2 * seat, 2, axis=1)
        bias = lax.dot_general(
            mine, bucket_hot, (((0,), (0,)), ((), ())), precision=lax.Precision.HIGHEST
        )
        bias = jnp.pad(bias, ((0, 6), (0, 0)))
        route = route_full[section]
        flat = route.reshape(-1)
        hot = (flat[:, None] == expert_index[None, :]).astype(jnp.int32)
        place = jnp.sum((jnp.cumsum(hot, axis=0) - hot) * hot, axis=1)
        spot = (flat * slots + place).reshape(rows, 2)
        placings = [
            (slot_index[:, None] == spot[:, c][None, :]).astype(bf16) for c in range(2)
        ]
        choose = (route[:, :, None] == expert_index[None, None, :]).astype(f32)
        sections.append(
            {
                "gain_mixer": gain_mixer,
                "gain_feed": gain_feed,
                "router": router,
                "bias": bias,
                "placings": placings,
                "placing": placings[0] + placings[1],
                "choose": choose,
                "weights": (
                    (core == section).astype(jnp.int32).reshape(1),
                    (inner_own, inner_other),
                    (outer_own, outer_other),
                ),
            }
        )

    def outgoing_of(p, values):
        return product(p["placing"], values).astype(bf16).reshape(experts, slots, width)

    def collect(p, returned):
        return [first_contract(p["placings"][c], returned) for c in range(2)]

    def with_line(values, line):
        line = line.reshape(experts, slots)
        high = lax.reduce_precision(line, 8, 7)
        line = jnp.concatenate([high, line - high], axis=1).astype(bf16)
        line = jnp.pad(line, ((0, 0), (0, width - 2 * slots)))
        return jnp.concatenate([values.reshape(experts, slots, width), line[:, None]], axis=1)

    def cut_line(values):
        line = values[:, slots, : 2 * slots].astype(f32)
        line = line[:, :slots] + line[:, slots:]
        return values[:, :slots].reshape(experts * slots, width), line.reshape(-1, 1)

    def normed_mixer(p, values):
        unit, _ = norm_parts(values.astype(f32))
        return (unit * p["gain_mixer"]).astype(bf16)

    def spread_heads(heads):
        mixed = exchange_near(heads.reshape(span, rows, PAIR))
        return jnp.transpose(mixed[:used], (1, 0, 2)).reshape(rows, width)

    def mixer(p, qkv, mixed, own):
        hidden = own.astype(f32) + product(mixed, p["output"])
        unit_feed, scale_feed = norm_parts(hidden)
        normed_feed = (unit_feed * p["gain_feed"]).astype(bf16)
        chances = jax.nn.softmax(product(normed_feed, p["router"]), axis=-1)
        chosen = jnp.sum(chances[:, None, :] * p["choose"], axis=-1)
        gate = chosen / jnp.sum(chosen, axis=1, keepdims=True)
        return {
            "own": own,
            "qkv": qkv,
            "mixed": mixed,
            "hidden": hidden,
            "unit_feed": unit_feed,
            "scale_feed": scale_feed,
            "normed_feed": normed_feed,
            "chances": chances,
            "chosen": chosen,
            "gate": gate,
        }

    def finish(cache, back):
        gate = cache["gate"]
        return (cache["hidden"] + (gate[:, 0:1] * back[0] + gate[:, 1:2] * back[1])).astype(bf16)

    def mixer_back(p, cache, delta_feed, delta_gate, delta_out, beside):
        chosen, chances = cache["chosen"], cache["chances"]
        total = jnp.sum(chosen, axis=1, keepdims=True)
        delta_chosen = delta_gate / total - jnp.sum(
            delta_gate * chosen, axis=1, keepdims=True
        ) / (total * total)
        delta_chances = jnp.sum(delta_chosen[:, :, None] * p["choose"], axis=1)
        delta_logits = (
            chances * (delta_chances - jnp.sum(chances * delta_chances, axis=-1, keepdims=True))
        ).astype(bf16)
        sum_router = first_contract(cache["normed_feed"], delta_logits)
        delta_feed = delta_feed + last_contract(delta_logits, p["router"])
        delta_hidden, sum_feed = norm_back(
            delta_feed, cache["unit_feed"], cache["scale_feed"], p["gain_feed"]
        )
        delta_hidden = delta_hidden + delta_out
        delta_branch = delta_hidden.astype(bf16)
        delta_mixed = last_contract(delta_branch, p["output"]).astype(bf16)
        delta_heads = exchange_near(by_pairs(delta_mixed)).reshape(SEQ_LEN, PAIR)
        beside = after(beside, delta_heads)
        sum_output = first_contract(cache["mixed"], delta_branch)
        delta_qkv, line = attend_back(cache["qkv"], p["bias"], delta_heads)
        parts = exchange_near(delta_qkv.reshape(span, rows, lanes))
        parts = jnp.transpose(parts[:used].reshape(used, rows, 3, PAIR), (1, 2, 0, 3))
        delta_normed = last_contract(parts.reshape(rows, 3 * width), p["qkv"])
        unit, scale = norm_parts(cache["own"].astype(f32))
        delta_in, sum_mixer = norm_back(delta_normed, unit, scale, p["gain_mixer"])
        if "attention" in p:
            heads_part = last_contract(delta_qkv, p["attention"])
            sum_mixer = jnp.sum(heads_part * norm_parts(cache["full"].astype(f32))[0], axis=0)
        delta_in = (delta_in + delta_hidden).astype(bf16)
        sum_attention = first_contract(cache["normed"](delta_qkv), delta_qkv)
        sum_table = lax.dot_general(
            bucket_hot, line[:2], (((1,), (1,)), ((), ())), precision=lax.Precision.HIGHEST
        )
        sum_table = lax.dynamic_update_slice_in_dim(
            jnp.zeros((BUCKETS, 2 * span), f32), sum_table, 2 * seat, axis=1
        )[:, :HEADS]
        blocks = jnp.concatenate(
            [
                sum_mixer.reshape(devices, share),
                sum_feed.reshape(devices, share),
                sum_router.reshape(devices, share * experts),
                sum_table.reshape(devices, table_share),
                jnp.zeros((devices, small_pad), f32),
            ],
            axis=1,
        ).reshape(devices, small_rows, lanes)
        sums = jnp.concatenate([sum_attention.reshape(devices, share, lanes), blocks], axis=1)
        return delta_in, sums, sum_output, beside, parts

    def half_columns(sums):
        mine, theirs = own_of((sums[:, : width // 2], sums[:, width // 2 :]))
        return mine + swap(theirs.astype(bf16)).astype(f32)

    p0, p1 = sections
    normed0 = normed_mixer(p0, full_first)
    qkv0 = product(normed0, attention_first).astype(bf16)
    mixed0 = spread_heads(attend(qkv0, p0["bias"]))
    p0["output"], p1["output"] = to_sections(after(dense_own[:, 3 * width :], mixed0))
    cache0 = mixer(p0, qkv0, mixed0, context)
    cache0["normed"], cache0["full"] = lambda _: normed0, full_first
    p0["attention"] = attention_first
    outgoing0 = [outgoing_of(p0, cache0["normed_feed"]), outgoing_of(p1, target)]
    arrived0 = exchange(jnp.concatenate(outgoing0, axis=1))
    arrived_target = arrived0[:, slots:].reshape(experts * slots, width)
    arrived0 = arrived0[:, :slots].reshape(experts * slots, width)
    activated0, slope0, result0 = expert_call(
        forward_kernel, [arrived0], [], p0["weights"], 2, 1
    )
    returned0 = exchange(result0.reshape(experts, slots, width)).reshape(-1, width)
    p0["qkv"], p1["qkv"] = to_sections(dense_own[:, : 3 * width])
    back0 = collect(p0, returned0)
    output0 = finish(cache0, back0)

    qkv1 = product(normed_mixer(p1, output0), p1["qkv"]).astype(bf16)
    qkv1 = exchange_near(
        three_by_pairs(qkv1[:, :width], qkv1[:, width : 2 * width], qkv1[:, 2 * width :])
    ).reshape(SEQ_LEN, lanes)
    cache1 = mixer(p1, qkv1, spread_heads(attend(qkv1, p1["bias"])), output0)
    gate1 = cache1["gate"]
    gate_slots = sum(
        jnp.sum(p1["placings"][c].astype(f32) * gate1[:, c][None, :], axis=1) for c in range(2)
    )
    outgoing1 = outgoing_of(p1, cache1["normed_feed"])
    arrived1, gate_slots = cut_line(exchange(with_line(outgoing1, gate_slots)))
    delta1 = (gate_slots * arrived_target.astype(f32)).astype(bf16)
    full_second = gather_near(after(output0, arrived1))
    activated1, before1, result1, leaving1 = expert_call(
        both_kernel, [arrived1, delta1], [], p1["weights"], 2, 2
    )
    cache1["normed"] = lambda later: normed_mixer(p1, after(full_second, later))
    leaving1 = after(leaving1, full_second)
    inner_gate = jnp.sum(arrived_target.astype(f32) * result1.astype(f32), axis=-1)
    home1, inner_gate = cut_line(exchange(with_line(leaving1, inner_gate)))
    home1 = collect(p1, home1)
    delta_gate1 = jnp.stack(
        [jnp.sum(p1["placings"][c].astype(f32) * inner_gate, axis=0) for c in range(2)], axis=1
    )
    delta_in1, sums1, sum_output1, result1, _ = mixer_back(
        p1, cache1, home1[0] + home1[1], delta_gate1, target.astype(f32), result1
    )
    back1 = collect(p1, exchange(result1.reshape(experts, slots, width)).reshape(-1, width))
    output1 = finish(cache1, back1)

    delta_out0 = delta_in1.astype(f32)
    gate0 = cache0["gate"]
    delta_back = [(gate0[:, c : c + 1] * delta_out0).astype(bf16) for c in range(2)]
    outgoing = product(p0["placings"][0], delta_back[0]) + product(p0["placings"][1], delta_back[1])
    arrived_delta = exchange(
        outgoing.astype(bf16).reshape(experts, slots, width)
    ).reshape(-1, width)
    output_half1 = lax.psum_scatter(
        half_columns(sum_output1), "dp", scatter_dimension=0, tiled=True
    )
    before0, leaving0 = expert_call(
        backward_kernel, [arrived_delta], [slope0], p0["weights"], 1, 1
    )
    home0 = collect(p0, exchange(leaving0.reshape(experts, slots, width)).reshape(-1, width))
    delta_gate0 = jnp.stack([jnp.sum(delta_out0 * back0[c], axis=-1) for c in range(2)], axis=1)
    delta_in0, sums0, sum_output0, _, parts0 = mixer_back(
        p0, cache0, home0[0] + home0[1], delta_gate0, delta_out0, result0
    )
    output_half0 = half_columns(sum_output0).astype(bf16).reshape(devices, share, width // 2)

    operands0 = (activated0, arrived_delta, arrived0, before0)
    operands1 = (activated1, delta1, arrived1, before1)
    joined = []
    for left, right in zip(operands0, operands1):
        mine, theirs = own_of((left, right))
        joined.append(jnp.concatenate([mine, swap(theirs)], axis=0))
    grad_outer = first_contract(joined[0], joined[1])
    grad_inner = first_contract(joined[2], joined[3])

    mine, theirs = own_of((sums0, sums1))
    sums = (mine + swap(theirs.astype(bf16)).astype(f32)).astype(bf16)
    sums = exchange(after(jnp.concatenate([sums, output_half0], axis=1), parts0))
    attention_sums = add_pairs(sums, span, share)
    sums = sums[:, share:].astype(f32)
    output_half0 = jnp.sum(sums[:, small_rows:], axis=0)
    small_sums = jnp.sum(sums[:, :small_rows], axis=0).reshape(-1)
    mine, theirs = own_of((output_half0, output_half1))
    other = swap(theirs)
    output_sums = jnp.concatenate(
        [jnp.where(zero, mine, other), jnp.where(zero, other, mine)], axis=1
    )
    totals = [small_sums[:share], small_sums[share : 2 * share]]
    totals.append(small_sums[2 * share : (2 + experts) * share].reshape(share, experts))
    end = (2 + experts) * share
    totals.append(small_sums[end : end + table_share])

    def by_micro(first, second):
        mine, theirs = own_of((first, second))
        other = swap(theirs)
        return jnp.stack([jnp.where(zero, mine, other), jnp.where(zero, other, mine)])[None]

    return (
        by_micro(output0, output1),
        by_micro(delta_in0, delta_in1),
        attention_sums[0][None],
        attention_sums[1][None],
        attention_sums[2][None],
        output_sums[None],
        totals[0][None],
        totals[1][None],
        totals[2][None],
        totals[3][None],
        grad_inner[None, None],
        grad_outer[None, None],
    )


def solution(mesh):
    in_specs = (
        P(None, "dp", None),
        P(None, "dp", None),
        P("section", None, "dp", None),
        P(),
        P("section", "dp", None),
        P("section", "dp", None),
        P("section", "dp", None),
        P("section", "dp", None),
        P("section", "dp"),
        P("section", "dp"),
        P("section", "dp", None),
        P("section", "dp"),
        P("section", "dp", None, None),
        P("section", "dp", None, None),
    )
    out_specs = (
        P("section", None, "dp", None),
        P("section", None, "dp", None),
        P("section", "dp", None),
        P("section", "dp", None),
        P("section", "dp", None),
        P("section", "dp", None),
        P("section", "dp"),
        P("section", "dp"),
        P("section", "dp", None),
        P("section", "dp"),
        P("section", "dp", None, None),
        P("section", "dp", None, None),
    )
    return jax.shard_map(
        on_device, mesh=mesh, in_specs=in_specs, out_specs=out_specs, check_vma=False
    )
```

```python
import functools

import jax
import jax.numpy as jnp
from jax import lax
from jax.experimental import pallas as pl
from jax.experimental.pallas import tpu as pltpu
from jax.sharding import PartitionSpec as P

HEADS = 12
HEAD_DIM = 64
BUCKETS = 32
SEQ_LEN = 1024

PAIR = 2 * HEAD_DIM
TILE = 256
BLOCKS = SEQ_LEN // TILE
REACH = SEQ_LEN + TILE

epsilon = 1e-06
score_scale = 0.125
bf16 = jnp.bfloat16
f32 = jnp.float32


def product(left, right):
    return jnp.dot(left, right, preferred_element_type=f32)


def first_contract(left, right):
    return lax.dot_general(left, right, (((0,), (0,)), ((), ())), preferred_element_type=f32)


def last_contract(left, right):
    return lax.dot_general(left, right, (((1,), (1,)), ((), ())), preferred_element_type=f32)


def norm_parts(values):
    scale = lax.rsqrt(jnp.mean(values * values, axis=-1, keepdims=True) + epsilon)
    return (values * scale, scale)


def norm_back(delta_out, unit, scale, gain):
    inner = delta_out * gain
    delta_in = scale * (inner - unit * jnp.mean(inner * unit, axis=-1, keepdims=True))
    return (delta_in, jnp.sum(delta_out * unit, axis=0))


def bias_tile(bias_ref, head, step):
    start = SEQ_LEN - TILE - TILE * step
    line = bias_ref[head : head + 1, start : start + 2 * TILE]
    spread = jnp.broadcast_to(line, (TILE, 2 * TILE))
    return pltpu.roll(spread, TILE + 1, 1, stride=1, stride_axis=0)[:, :TILE]


def block_scores(qkv_ref, tiles, head, block):
    low = HEAD_DIM * head
    seen = TILE * (block + 1)
    query = qkv_ref[TILE * block : seen, low : low + HEAD_DIM]
    key = qkv_ref[0:seen, PAIR + low : PAIR + low + HEAD_DIM]
    raw = last_contract(query, key) * score_scale
    bias = jnp.concatenate([tiles[head, block - j] for j in range(block + 1)], axis=1)
    rows = lax.broadcasted_iota(jnp.int32, (TILE, seen), 0) + TILE * block
    columns = lax.broadcasted_iota(jnp.int32, (TILE, seen), 1)
    scores = jnp.where(columns <= rows, raw + bias, -1e30)
    top = jnp.max(scores, axis=-1, keepdims=True)
    weights = jnp.exp(scores - top)
    weights = weights * (1.0 / jnp.sum(weights, axis=-1, keepdims=True))
    return query, key, weights


def attend_kernel(qkv_ref, bias_ref, out_ref, tiles):
    for head in range(2):
        low = HEAD_DIM * head
        for step in range(BLOCKS):
            tiles[head, step] = bias_tile(bias_ref, head, step)
        for block in range(BLOCKS):
            seen = TILE * (block + 1)
            _, _, weights = block_scores(qkv_ref, tiles, head, block)
            value = qkv_ref[0:seen, 2 * PAIR + low : 2 * PAIR + low + HEAD_DIM]
            out_ref[TILE * block : seen, low : low + HEAD_DIM] = product(
                weights.astype(bf16), value
            ).astype(bf16)


def attend_back_kernel(qkv_ref, bias_ref, delta_ref, grad_ref, line_ref, tiles, sums, keys, values):
    line_ref[...] = jnp.zeros_like(line_ref)
    for head in range(2):
        low = HEAD_DIM * head
        for step in range(BLOCKS):
            tiles[head, step] = bias_tile(bias_ref, head, step)
            sums[step] = jnp.zeros((TILE, TILE), f32)
        keys[...] = jnp.zeros_like(keys)
        values[...] = jnp.zeros_like(values)
        for block in range(BLOCKS):
            seen = TILE * (block + 1)
            query, key, weights = block_scores(qkv_ref, tiles, head, block)
            value = qkv_ref[0:seen, 2 * PAIR + low : 2 * PAIR + low + HEAD_DIM]
            delta = delta_ref[TILE * block : seen, low : low + HEAD_DIM]
            delta_weights = last_contract(delta, value)
            inner = jnp.sum(weights * delta_weights, axis=-1, keepdims=True)
            delta_scores = (weights * (delta_weights - inner)).astype(bf16)
            grad_ref[TILE * block : seen, low : low + HEAD_DIM] = (
                product(delta_scores, key) * score_scale
            ).astype(bf16)
            keys[0:seen, :] += first_contract(delta_scores, query)
            values[0:seen, :] += first_contract(weights.astype(bf16), delta)
            for j in range(block + 1):
                sums[block - j] += delta_scores[:, TILE * j : TILE * (j + 1)].astype(f32)
        grad_ref[:, PAIR + low : PAIR + low + HEAD_DIM] = (keys[...] * score_scale).astype(bf16)
        grad_ref[:, 2 * PAIR + low : 2 * PAIR + low + HEAD_DIM] = values[...].astype(bf16)
        for step in range(BLOCKS):
            start = SEQ_LEN - TILE - TILE * step
            eight = jnp.zeros((8, 2 * TILE), f32)
            for group in range(TILE // 8):
                part = sums[step, 8 * group : 8 * group + 8, :]
                part = jnp.concatenate([part, jnp.zeros_like(part)], axis=1)
                eight = eight + pltpu.roll(part, TILE - 1 - 8 * group, 1)
            line = eight[0:1]
            for row in range(1, 8):
                line = line + pltpu.roll(eight, 2 * TILE - row, 1)[row : row + 1]
            line_ref[head : head + 1, start : start + 2 * TILE] += line


def attend(qkv, bias):
    return pl.pallas_call(
        attend_kernel,
        out_shape=jax.ShapeDtypeStruct((SEQ_LEN, PAIR), bf16),
        in_specs=[pl.BlockSpec(memory_space=pltpu.VMEM)] * 2,
        out_specs=pl.BlockSpec(memory_space=pltpu.VMEM),
        scratch_shapes=[pltpu.VMEM((2, BLOCKS, TILE, TILE), f32)],
        compiler_params=pltpu.CompilerParams(vmem_limit_bytes=40 * 1024 * 1024),
        cost_estimate=pl.CostEstimate(
            flops=48 * SEQ_LEN * SEQ_LEN * PAIR,
            bytes_accessed=SEQ_LEN * PAIR * 8,
            transcendentals=SEQ_LEN * SEQ_LEN,
        ),
    )(qkv, bias)


def attend_back(qkv, bias, delta):
    return pl.pallas_call(
        attend_back_kernel,
        out_shape=(
            jax.ShapeDtypeStruct((SEQ_LEN, 3 * PAIR), bf16),
            jax.ShapeDtypeStruct((8, REACH), f32),
        ),
        in_specs=[pl.BlockSpec(memory_space=pltpu.VMEM)] * 3,
        out_specs=(pl.BlockSpec(memory_space=pltpu.VMEM),) * 2,
        scratch_shapes=[
            pltpu.VMEM((2, BLOCKS, TILE, TILE), f32),
            pltpu.VMEM((BLOCKS, TILE, TILE), f32),
            pltpu.VMEM((SEQ_LEN, HEAD_DIM), f32),
            pltpu.VMEM((SEQ_LEN, HEAD_DIM), f32),
        ],
        compiler_params=pltpu.CompilerParams(vmem_limit_bytes=40 * 1024 * 1024),
        cost_estimate=pl.CostEstimate(
            flops=96 * SEQ_LEN * SEQ_LEN * PAIR,
            bytes_accessed=SEQ_LEN * PAIR * 16,
            transcendentals=SEQ_LEN * SEQ_LEN,
        ),
    )(qkv, bias, delta)


CHUNK = 512
PART = 256
gelu_root = 0.7978845608028654
gelu_cube = 0.044715


def gelu_parts(before):
    square = before * before
    bend = jnp.tanh(gelu_root * before * (1.0 + gelu_cube * square))
    half = 0.5 * (1.0 + bend)
    slope = half + (0.5 * gelu_root) * before * (1.0 - bend * bend) * (
        1.0 + (3.0 * gelu_cube) * square
    )
    return before * half, slope


def add_product(total, value):
    @pl.when(pl.program_id(0) == 0)
    def _():
        total[...] = value

    @pl.when(pl.program_id(0) > 0)
    def _():
        total[...] += value


def pick(choice_ref, refs):
    return jnp.where(choice_ref[0] == 1, refs[0][...], refs[1][...])


def parts_of(value, axis):
    return jnp.split(value, CHUNK // PART, axis=axis)


def forward_kernel(
    choice_ref, in_ref, inner_0, inner_1, outer_0, outer_1, act_ref, slope_ref, out_ref, total
):
    inner = pick(choice_ref, (inner_0, inner_1))
    outer = pick(choice_ref, (outer_0, outer_1))
    act, slope = gelu_parts(product(in_ref[...], inner))
    act = act.astype(bf16)
    act_ref[...] = act
    slope_ref[...] = slope.astype(bf16)
    add_product(total, product(act, outer))

    @pl.when(pl.program_id(0) == pl.num_programs(0) - 1)
    def _():
        out_ref[...] = total[...].astype(bf16)


def backward_kernel(
    choice_ref, delta_ref, slope_ref, inner_0, inner_1, outer_0, outer_1, pre_ref, out_ref, total
):
    inner = pick(choice_ref, (inner_0, inner_1))
    outer = pick(choice_ref, (outer_0, outer_1))
    pre = last_contract(delta_ref[...], outer) * slope_ref[...].astype(f32)
    pre = pre.astype(bf16)
    pre_ref[...] = pre
    add_product(total, last_contract(pre, inner))

    @pl.when(pl.program_id(0) == pl.num_programs(0) - 1)
    def _():
        out_ref[...] = total[...].astype(bf16)


def both_kernel(
    choice_ref,
    in_ref,
    delta_ref,
    inner_0,
    inner_1,
    outer_0,
    outer_1,
    act_ref,
    pre_ref,
    out_ref,
    back_ref,
    total,
    back,
):
    values, delta = in_ref[...], delta_ref[...]
    inner = parts_of(pick(choice_ref, (inner_0, inner_1)), 1)
    outer = parts_of(pick(choice_ref, (outer_0, outer_1)), 0)
    befores = [product(values, part) for part in inner]
    deltas = [last_contract(delta, part) for part in outer]
    value, value_back = 0.0, 0.0
    for i, before in enumerate(befores):
        act, slope = gelu_parts(before)
        act = act.astype(bf16)
        act_ref[:, PART * i : PART * (i + 1)] = act
        pre = (deltas[i] * slope).astype(bf16)
        pre_ref[:, PART * i : PART * (i + 1)] = pre
        value_back = value_back + last_contract(pre, inner[i])
        value = value + product(act, outer[i])
    add_product(back, value_back)
    add_product(total, value)

    @pl.when(pl.program_id(0) == pl.num_programs(0) - 1)
    def _():
        out_ref[...] = total[...].astype(bf16)
        back_ref[...] = back[...].astype(bf16)


def expert_call(kernel, held, streamed, weights, wide, narrow):
    choice, inner, outer = weights
    rows, width = held[0].shape
    hidden = inner[0].shape[1]
    whole = pl.BlockSpec((rows, width), lambda i, c: (0, 0))
    cut = pl.BlockSpec((rows, CHUNK), lambda i, c: (0, i))
    return pl.pallas_call(
        kernel,
        grid_spec=pltpu.PrefetchScalarGridSpec(
            num_scalar_prefetch=1,
            grid=(hidden // CHUNK,),
            in_specs=[whole] * len(held)
            + [cut] * len(streamed)
            + [
                pl.BlockSpec((width, CHUNK), lambda i, c: (0, i * c[0])),
                pl.BlockSpec((width, CHUNK), lambda i, c: (0, i * (1 - c[0]))),
                pl.BlockSpec((CHUNK, width), lambda i, c: (i * c[0], 0)),
                pl.BlockSpec((CHUNK, width), lambda i, c: (i * (1 - c[0]), 0)),
            ],
            out_specs=[cut] * wide + [whole] * narrow,
            scratch_shapes=[pltpu.VMEM((rows, width), f32)] * narrow,
        ),
        out_shape=[jax.ShapeDtypeStruct((rows, hidden), bf16)] * wide
        + [jax.ShapeDtypeStruct((rows, width), bf16)] * narrow,
        compiler_params=pltpu.CompilerParams(vmem_limit_bytes=48 * 1024 * 1024),
        cost_estimate=pl.CostEstimate(
            flops=12 * narrow * rows * width * hidden,
            bytes_accessed=4 * width * hidden + 2 * rows * hidden * (wide + len(streamed)),
            transcendentals=rows * hidden,
        ),
    )(choice, *held, *streamed, *inner, *outer)


def add_pairs_kernel(span, in_ref, *out_refs):
    share, width = out_refs[0].shape
    for part, out_ref in enumerate(out_refs):
        for pair in range(width // PAIR):
            total = 0.0
            for source in range(pair, in_ref.shape[0], span):
                block = in_ref[source, 0:share, PAIR * part : PAIR * (part + 1)]
                total = total + block.astype(f32)
            out_ref[:, PAIR * pair : PAIR * (pair + 1)] = total


def add_pairs(blocks, span, share):
    return pl.pallas_call(
        functools.partial(add_pairs_kernel, span),
        out_shape=[jax.ShapeDtypeStruct((share, HEADS * HEAD_DIM), f32)] * 3,
        in_specs=[pl.BlockSpec(memory_space=pltpu.VMEM)],
        out_specs=[pl.BlockSpec(memory_space=pltpu.VMEM)] * 3,
        compiler_params=pltpu.CompilerParams(vmem_limit_bytes=32 * 1024 * 1024),
    )(blocks)


def on_device(
    tokens,
    cotangent,
    routes,
    rel_bucket,
    query_weight,
    key_weight,
    value_weight,
    output_weight,
    mixer_gain,
    feed_gain,
    router_weight,
    bias_table,
    expert_in,
    expert_out,
):
    core = lax.axis_index("section")
    place_dp = lax.axis_index("dp")
    devices = lax.axis_size("dp")
    micro = tokens.shape[0]
    rows = tokens.shape[1]
    width = tokens.shape[2]
    span = SEQ_LEN // rows
    seat = place_dp % span
    slots = max(2, 4 * rows // devices)
    experts = devices
    share = width // devices
    table_share = BUCKETS * HEADS // devices
    used = HEADS // 2
    lanes = 3 * PAIR
    circles = [list(range(i, i + span)) for i in range(0, devices, span)]
    zero = core == 0

    def swap(value):
        return lax.ppermute(value, "section", [(0, 1), (1, 0)])

    def to_sections(own):
        other = swap(own)
        return jnp.where(zero, own, other), jnp.where(zero, other, own)

    def own_of(values):
        return jnp.where(zero, values[0], values[1]), jnp.where(zero, values[1], values[0])

    def after(value, first):
        element = first[(0,) * first.ndim].astype(f32)
        return value + (element * 0.0).astype(value.dtype)

    def exchange(value):
        return lax.all_to_all(value, "dp", 0, 0, tiled=True)

    def exchange_near(value):
        return lax.all_to_all(value, "dp", 0, 0, tiled=True, axis_index_groups=circles)

    def gather_near(value):
        spread = jnp.broadcast_to(value[None], (span,) + value.shape)
        return exchange_near(spread).reshape(SEQ_LEN, -1)

    def by_pairs(values):
        count = values.shape[0]
        padded = jnp.pad(values, ((0, 0), (0, span * PAIR - width)))
        return jnp.transpose(padded.reshape(count, span, PAIR), (1, 0, 2))

    def three_by_pairs(left, middle, right):
        return jnp.concatenate([by_pairs(left), by_pairs(middle), by_pairs(right)], axis=2)

    context = jnp.where(zero, tokens[0], tokens[1])
    target = jnp.where(zero, cotangent[0], cotangent[1])
    full_first = gather_near(context)

    dense_own = lax.all_gather(
        jnp.concatenate(
            [query_weight[0], key_weight[0], value_weight[0], output_weight[0]], axis=1
        ),
        "dp",
        axis=0,
        tiled=True,
    )
    small = jnp.concatenate(
        [mixer_gain[0], feed_gain[0], router_weight[0].reshape(-1), bias_table[0]]
    )
    small_rows = 8 * (-(-small.shape[0] // (8 * lanes)))
    small_pad = small_rows * lanes - small.shape[0]
    small = jnp.pad(small, (0, small_pad)).reshape(1, small_rows, lanes)
    half = share // 2
    pairs_weight = three_by_pairs(query_weight[0], key_weight[0], value_weight[0])
    passed = lax.ppermute(pairs_weight[:, half:], "section", [(0, 1)])
    pairs_weight = jnp.concatenate(
        [
            jnp.where(zero, pairs_weight[:, :half], passed),
            jnp.broadcast_to(small, (span,) + small.shape[1:]),
        ],
        axis=1,
    )
    pairs_weight = jnp.concatenate([pairs_weight] * (devices // span), axis=0)
    pairs_weight, full_first = lax.optimization_barrier((pairs_weight, full_first))
    front = to_sections(exchange(pairs_weight))
    attention_first = jnp.concatenate([front[0][:, :half], front[1][:, :half]], axis=1).reshape(
        width, lanes
    )
    inner_own, outer_own = expert_in[0, 0], expert_out[0, 0]
    inner_other, outer_other = swap(inner_own), swap(outer_own)
    route_mine, route_theirs = own_of((routes[0, 0], routes[0, 1]))
    route_other = swap(route_theirs)
    route_full = (
        jnp.where(zero, route_mine, route_other),
        jnp.where(zero, route_other, route_mine),
    )

    bucket_numbers = jnp.arange(BUCKETS, dtype=jnp.int32)
    reverse = jnp.concatenate([rel_bucket[::-1], jnp.full((TILE,), -1, jnp.int32)])
    bucket_hot = (bucket_numbers[:, None] == reverse[None, :]).astype(f32)
    slot_index = jnp.arange(experts * slots, dtype=jnp.int32)
    expert_index = jnp.arange(experts, dtype=jnp.int32)

    sections = []
    for section in range(2):
        flat_small = front[section][:, half:].reshape(devices, small_rows * lanes)
        cut = [share, 2 * share, (2 + experts) * share, (2 + experts) * share + table_share]
        gain_mixer = flat_small[:, : cut[0]].reshape(width).astype(f32)
        gain_feed = flat_small[:, cut[0] : cut[1]].reshape(width).astype(f32)
        router = flat_small[:, cut[1] : cut[2]].reshape(width, experts)
        table = flat_small[:, cut[2] : cut[3]].reshape(BUCKETS, HEADS).astype(f32)
        table = jnp.pad(table, ((0, 0), (0, 2 * span - HEADS)))
        mine = lax.dynamic_slice_in_dim(table, 2 * seat, 2, axis=1)
        bias = lax.dot_general(
            mine, bucket_hot, (((0,), (0,)), ((), ())), precision=lax.Precision.HIGHEST
        )
        bias = jnp.pad(bias, ((0, 6), (0, 0)))
        route = route_full[section]
        flat = route.reshape(-1)
        hot = (flat[:, None] == expert_index[None, :]).astype(jnp.int32)
        place = jnp.sum((jnp.cumsum(hot, axis=0) - hot) * hot, axis=1)
        spot = (flat * slots + place).reshape(rows, 2)
        placings = [
            (slot_index[:, None] == spot[:, c][None, :]).astype(bf16) for c in range(2)
        ]
        choose = (route[:, :, None] == expert_index[None, None, :]).astype(f32)
        sections.append(
            {
                "gain_mixer": gain_mixer,
                "gain_feed": gain_feed,
                "router": router,
                "bias": bias,
                "placings": placings,
                "placing": placings[0] + placings[1],
                "choose": choose,
                "weights": (
                    (core == section).astype(jnp.int32).reshape(1),
                    (inner_own, inner_other),
                    (outer_own, outer_other),
                ),
            }
        )

    def outgoing_of(p, values):
        return product(p["placing"], values).astype(bf16).reshape(experts, slots, width)

    def collect(p, returned):
        return [first_contract(p["placings"][c], returned) for c in range(2)]

    def with_line(values, line):
        line = line.reshape(experts, slots)
        high = lax.reduce_precision(line, 8, 7)
        line = jnp.concatenate([high, line - high], axis=1).astype(bf16)
        line = jnp.pad(line, ((0, 0), (0, width - 2 * slots)))
        return jnp.concatenate([values.reshape(experts, slots, width), line[:, None]], axis=1)

    def cut_line(values):
        line = values[:, slots, : 2 * slots].astype(f32)
        line = line[:, :slots] + line[:, slots:]
        return values[:, :slots].reshape(experts * slots, width), line.reshape(-1, 1)

    def normed_mixer(p, values):
        unit, _ = norm_parts(values.astype(f32))
        return (unit * p["gain_mixer"]).astype(bf16)

    def spread_heads(heads):
        mixed = exchange_near(heads.reshape(span, rows, PAIR))
        return jnp.transpose(mixed[:used], (1, 0, 2)).reshape(rows, width)

    def mixer(p, qkv, mixed, own):
        hidden = own.astype(f32) + product(mixed, p["output"])
        unit_feed, scale_feed = norm_parts(hidden)
        normed_feed = (unit_feed * p["gain_feed"]).astype(bf16)
        chances = jax.nn.softmax(product(normed_feed, p["router"]), axis=-1)
        chosen = jnp.sum(chances[:, None, :] * p["choose"], axis=-1)
        gate = chosen / jnp.sum(chosen, axis=1, keepdims=True)
        return {
            "own": own,
            "qkv": qkv,
            "mixed": mixed,
            "hidden": hidden,
            "unit_feed": unit_feed,
            "scale_feed": scale_feed,
            "normed_feed": normed_feed,
            "chances": chances,
            "chosen": chosen,
            "gate": gate,
        }

    def finish(cache, back):
        gate = cache["gate"]
        return (cache["hidden"] + (gate[:, 0:1] * back[0] + gate[:, 1:2] * back[1])).astype(bf16)

    def mixer_back(p, cache, delta_feed, delta_gate, delta_out, beside):
        chosen, chances = cache["chosen"], cache["chances"]
        total = jnp.sum(chosen, axis=1, keepdims=True)
        delta_chosen = delta_gate / total - jnp.sum(
            delta_gate * chosen, axis=1, keepdims=True
        ) / (total * total)
        delta_chances = jnp.sum(delta_chosen[:, :, None] * p["choose"], axis=1)
        delta_logits = (
            chances * (delta_chances - jnp.sum(chances * delta_chances, axis=-1, keepdims=True))
        ).astype(bf16)
        sum_router = first_contract(cache["normed_feed"], delta_logits)
        delta_feed = delta_feed + last_contract(delta_logits, p["router"])
        delta_hidden, sum_feed = norm_back(
            delta_feed, cache["unit_feed"], cache["scale_feed"], p["gain_feed"]
        )
        delta_hidden = delta_hidden + delta_out
        delta_branch = delta_hidden.astype(bf16)
        delta_mixed = last_contract(delta_branch, p["output"]).astype(bf16)
        delta_heads = exchange_near(by_pairs(delta_mixed)).reshape(SEQ_LEN, PAIR)
        beside = after(beside, delta_heads)
        sum_output = first_contract(cache["mixed"], delta_branch)
        delta_qkv, line = attend_back(cache["qkv"], p["bias"], delta_heads)
        parts = exchange_near(delta_qkv.reshape(span, rows, lanes))
        parts = jnp.transpose(parts[:used].reshape(used, rows, 3, PAIR), (1, 2, 0, 3))
        delta_normed = last_contract(parts.reshape(rows, 3 * width), p["qkv"])
        unit, scale = norm_parts(cache["own"].astype(f32))
        delta_in, sum_mixer = norm_back(delta_normed, unit, scale, p["gain_mixer"])
        if "attention" in p:
            heads_part = last_contract(delta_qkv, p["attention"])
            sum_mixer = jnp.sum(heads_part * norm_parts(cache["full"].astype(f32))[0], axis=0)
        delta_in = (delta_in + delta_hidden).astype(bf16)
        sum_attention = first_contract(cache["normed"](delta_qkv), delta_qkv)
        sum_table = lax.dot_general(
            bucket_hot, line[:2], (((1,), (1,)), ((), ())), precision=lax.Precision.HIGHEST
        )
        sum_table = lax.dynamic_update_slice_in_dim(
            jnp.zeros((BUCKETS, 2 * span), f32), sum_table, 2 * seat, axis=1
        )[:, :HEADS]
        blocks = jnp.concatenate(
            [
                sum_mixer.reshape(devices, share),
                sum_feed.reshape(devices, share),
                sum_router.reshape(devices, share * experts),
                sum_table.reshape(devices, table_share),
                jnp.zeros((devices, small_pad), f32),
            ],
            axis=1,
        ).reshape(devices, small_rows, lanes)
        sums = jnp.concatenate([sum_attention.reshape(devices, share, lanes), blocks], axis=1)
        return delta_in, sums, sum_output, beside, parts

    def half_columns(sums):
        mine, theirs = own_of((sums[:, : width // 2], sums[:, width // 2 :]))
        return mine + swap(theirs.astype(bf16)).astype(f32)

    p0, p1 = sections
    normed0 = normed_mixer(p0, full_first)
    qkv0 = product(normed0, attention_first).astype(bf16)
    mixed0 = spread_heads(attend(qkv0, p0["bias"]))
    p0["output"], p1["output"] = to_sections(after(dense_own[:, 3 * width :], mixed0))
    cache0 = mixer(p0, qkv0, mixed0, context)
    cache0["normed"], cache0["full"] = lambda _: normed0, full_first
    p0["attention"] = attention_first
    outgoing0 = [outgoing_of(p0, cache0["normed_feed"]), outgoing_of(p1, target)]
    arrived0 = exchange(jnp.concatenate(outgoing0, axis=1))
    arrived_target = arrived0[:, slots:].reshape(experts * slots, width)
    arrived0 = arrived0[:, :slots].reshape(experts * slots, width)
    activated0, slope0, result0 = expert_call(
        forward_kernel, [arrived0], [], p0["weights"], 2, 1
    )
    returned0 = exchange(result0.reshape(experts, slots, width)).reshape(-1, width)
    p0["qkv"], p1["qkv"] = to_sections(dense_own[:, : 3 * width])
    back0 = collect(p0, returned0)
    output0 = finish(cache0, back0)

    qkv1 = product(normed_mixer(p1, output0), p1["qkv"]).astype(bf16)
    qkv1 = exchange_near(
        three_by_pairs(qkv1[:, :width], qkv1[:, width : 2 * width], qkv1[:, 2 * width :])
    ).reshape(SEQ_LEN, lanes)
    cache1 = mixer(p1, qkv1, spread_heads(attend(qkv1, p1["bias"])), output0)
    gate1 = cache1["gate"]
    gate_slots = sum(
        jnp.sum(p1["placings"][c].astype(f32) * gate1[:, c][None, :], axis=1) for c in range(2)
    )
    outgoing1 = outgoing_of(p1, cache1["normed_feed"])
    arrived1, gate_slots = cut_line(exchange(with_line(outgoing1, gate_slots)))
    delta1 = (gate_slots * arrived_target.astype(f32)).astype(bf16)
    full_second = gather_near(after(output0, arrived1))
    activated1, before1, result1, leaving1 = expert_call(
        both_kernel, [arrived1, delta1], [], p1["weights"], 2, 2
    )
    cache1["normed"] = lambda later: normed_mixer(p1, after(full_second, later))
    inner_gate = jnp.sum(arrived_target.astype(f32) * result1.astype(f32), axis=-1)
    inner_gate = after(inner_gate, full_second)
    home1, inner_gate = cut_line(exchange(with_line(leaving1, inner_gate)))
    home1 = collect(p1, home1)
    delta_gate1 = jnp.stack(
        [jnp.sum(p1["placings"][c].astype(f32) * inner_gate, axis=0) for c in range(2)], axis=1
    )
    delta_in1, sums1, sum_output1, result1, _ = mixer_back(
        p1, cache1, home1[0] + home1[1], delta_gate1, target.astype(f32), result1
    )
    back1 = collect(p1, exchange(result1.reshape(experts, slots, width)).reshape(-1, width))
    output1 = finish(cache1, back1)

    delta_out0 = delta_in1.astype(f32)
    gate0 = cache0["gate"]
    delta_back = [(gate0[:, c : c + 1] * delta_out0).astype(bf16) for c in range(2)]
    outgoing = product(p0["placings"][0], delta_back[0]) + product(p0["placings"][1], delta_back[1])
    arrived_delta = exchange(
        outgoing.astype(bf16).reshape(experts, slots, width)
    ).reshape(-1, width)
    output_half1 = lax.psum_scatter(
        half_columns(sum_output1), "dp", scatter_dimension=0, tiled=True
    )
    before0, leaving0 = expert_call(
        backward_kernel, [arrived_delta], [slope0], p0["weights"], 1, 1
    )
    home0 = collect(p0, exchange(leaving0.reshape(experts, slots, width)).reshape(-1, width))
    delta_gate0 = jnp.stack([jnp.sum(delta_out0 * back0[c], axis=-1) for c in range(2)], axis=1)
    delta_in0, sums0, sum_output0, _, parts0 = mixer_back(
        p0, cache0, home0[0] + home0[1], delta_gate0, delta_out0, result0
    )
    output_half0 = half_columns(sum_output0).astype(bf16).reshape(devices, share, width // 2)

    operands0 = (activated0, arrived_delta, arrived0, before0)
    operands1 = (activated1, delta1, arrived1, before1)
    joined = []
    for left, right in zip(operands0, operands1):
        mine, theirs = own_of((left, right))
        joined.append(jnp.concatenate([mine, swap(theirs)], axis=0))
    grad_outer = first_contract(joined[0], joined[1])
    grad_inner = first_contract(joined[2], joined[3])

    mine, theirs = own_of((sums0, sums1))
    sums = (mine + swap(theirs.astype(bf16)).astype(f32)).astype(bf16)
    sums = exchange(after(jnp.concatenate([sums, output_half0], axis=1), parts0))
    attention_sums = add_pairs(sums, span, share)
    sums = sums[:, share:].astype(f32)
    output_half0 = jnp.sum(sums[:, small_rows:], axis=0)
    small_sums = jnp.sum(sums[:, :small_rows], axis=0).reshape(-1)
    mine, theirs = own_of((output_half0, output_half1))
    other = swap(theirs)
    output_sums = jnp.concatenate(
        [jnp.where(zero, mine, other), jnp.where(zero, other, mine)], axis=1
    )
    totals = [small_sums[:share], small_sums[share : 2 * share]]
    totals.append(small_sums[2 * share : (2 + experts) * share].reshape(share, experts))
    end = (2 + experts) * share
    totals.append(small_sums[end : end + table_share])

    def by_micro(first, second):
        mine, theirs = own_of((first, second))
        other = swap(theirs)
        return jnp.stack([jnp.where(zero, mine, other), jnp.where(zero, other, mine)])[None]

    return (
        by_micro(output0, output1),
        by_micro(delta_in0, delta_in1),
        attention_sums[0][None],
        attention_sums[1][None],
        attention_sums[2][None],
        output_sums[None],
        totals[0][None],
        totals[1][None],
        totals[2][None],
        totals[3][None],
        grad_inner[None, None],
        grad_outer[None, None],
    )


def solution(mesh):
    in_specs = (
        P(None, "dp", None),
        P(None, "dp", None),
        P("section", None, "dp", None),
        P(),
        P("section", "dp", None),
        P("section", "dp", None),
        P("section", "dp", None),
        P("section", "dp", None),
        P("section", "dp"),
        P("section", "dp"),
        P("section", "dp", None),
        P("section", "dp"),
        P("section", "dp", None, None),
        P("section", "dp", None, None),
    )
    out_specs = (
        P("section", None, "dp", None),
        P("section", None, "dp", None),
        P("section", "dp", None),
        P("section", "dp", None),
        P("section", "dp", None),
        P("section", "dp", None),
        P("section", "dp"),
        P("section", "dp"),
        P("section", "dp", None),
        P("section", "dp"),
        P("section", "dp", None, None),
        P("section", "dp", None, None),
    )
    return jax.shard_map(
        on_device, mesh=mesh, in_specs=in_specs, out_specs=out_specs, check_vma=False
    )
```
